512 devices in a mesh: lag: 8 (over y_lo, core), space: 64 (over x, y_hi, z).
Axes of the slice: x: 4, y: 8 (y_hi: 2, y_lo: 4; y = y_hi * 4 + y_lo), z: 8, core: 2. Of those that a mesh axis runs over, the one named last changes fastest.
Arguments:
- states: bfloat16 [8, 80, 127, 8192], P('lag', None, None, 'space'), may hold values from -6 to 6
- obs_weights: bfloat16 [24, 127], replicated, may hold values from -0.5 to 0.5
- observations: float32 [24, 8192], P(None, 'space'), may hold values from -6 to 6
- obs_precision: float32 [24, 8192], P(None, 'space'), may hold values from 0.3 to 3
- resample_index: int32 [1024, 80], P('space'), may hold values from 0 to 79
- blend_weight: float32 [1024], P('space'), may hold values from 0.2 to 0.7
- stencil_region: int32 [8192], P('space'), may hold values from 0 to 1023, as said below
- stencil_weight: float32 [8192], P('space'), may hold values from 0.5 to 1
Outputs:
- analysis: bfloat16 [8, 80, 127, 8192], P('lag', None, None, 'space')
The draws below stay inside these ranges and needn't reach their ends.
Inputs may be any that keep to these rules, and one draw needn't show every extreme that they name: `resample_index`: each entry names one of the 80 members. `stencil_region`: column c lies in region c // 8; its entry is that region or the region before or after it; the first column of a region names the region before it and the last column the region after it, wherever those exist.
All inputs are finite; a program needn't handle non-finite values.
Results may differ from the reference program's by a relative error of at most 0.0012.
The reference program's roundings to bfloat16 on the way (of `transforms` and `column_maps`) count: a program that leaves them out, or rounds other values in their place, can miss the bound.
Values may be sent and summed in bfloat16 or wider, within the bound.
A program may use at most 64 MiB of HBM per device.

```python
import math
import jax
import jax.numpy as jnp
from jax import lax

M = 80
LEV = 127
NOBS = 24
COLS_REG = 8
NS_ITERS = 8
LAGS = 8
REGIONS = 1024
COLUMNS = 8192


def draw_stencil_region(key, part):
    column = jnp.arange(COLUMNS, dtype=jnp.int32)
    region = column // COLS_REG
    within = column % COLS_REG
    direction_sign = jax.random.randint(key, (COLUMNS,), 0, 2, dtype=jnp.int32) * 2 - 1
    direction_sign = jnp.where(within == 0, -1, jnp.where(within == COLS_REG - 1, 1, direction_sign))
    return jnp.clip(region + direction_sign, 0, REGIONS - 1).astype(jnp.int32)


def set_ends(entries, key, smallest, top_value):
    longest = entries.shape.index(max(entries.shape))
    spots = []
    for shift in (0, 1):
        where = [jax.random.randint(jax.random.fold_in(key, axis), (), 0, length) for axis, length in enumerate(entries.shape)]
        where[longest] = (where[longest] + shift) % entries.shape[longest]
        spots.append(tuple(where))
    return entries.at[spots[0]].set(smallest).at[spots[1]].set(top_value)


def levels(key, dims, pieces, smallest, largest):
    level = 1.0
    for axis_at, parts in pieces:
        draws = jax.random.uniform(jax.random.fold_in(jax.random.fold_in(key, 6), axis_at), (parts,), jnp.float32, smallest / len(pieces), largest / len(pieces))
        level = level * jnp.repeat(jnp.exp(draws), dims[axis_at] // parts).reshape((-1,) + (1,) * (len(dims) - 1 - axis_at))
    return level


def bell_draw(stream_key, shape, spread, reach, shards=(), kind=jnp.bfloat16):
    result = spread * jax.random.normal(stream_key, shape, jnp.float32)
    if shards:
        result = result * levels(stream_key, shape, shards, -0.22, 0.18)
    return jnp.clip(result, -reach, reach).astype(kind)


def setup_inputs(seed: int = 0) -> dict:
    streams_of = jax.random.split(jax.random.key(seed), 9)
    states = bell_draw(streams_of[0], (LAGS, M, LEV, COLUMNS), 1.0, 6.0, ((0, 8), (3, 64)))
    obs_weights = bell_draw(streams_of[1], (NOBS, LEV), LEV ** -0.5, 0.5)
    observations = bell_draw(streams_of[2], (NOBS, COLUMNS), 1.0, 6.0, ((1, 64),), jnp.float32)
    obs_precision = jnp.clip(jnp.exp(math.log(3.0) - 2.3025851 * jax.random.uniform(streams_of[3], (NOBS, COLUMNS), jnp.float32) ** levels(streams_of[3], (NOBS, COLUMNS), ((1, 64),), -0.2, 0.2)), 0.3, 3.0)
    resample_index = set_ends(jax.random.randint(streams_of[4], (REGIONS, M), 0, M), jax.random.fold_in(streams_of[4], 1), 0, M - 1).astype(jnp.int32)
    blend_weight = jnp.clip(0.2 + 0.5 * jax.random.uniform(streams_of[5], (REGIONS,), jnp.float32) ** levels(streams_of[5], (REGIONS,), ((0, 64),), -0.2, 0.2), 0.2, 0.7)
    stencil_region = draw_stencil_region(jax.random.fold_in(streams_of[8], 71), 0)
    stencil_weight = jnp.clip(0.5 + 0.5 * jax.random.uniform(streams_of[7], (COLUMNS,), jnp.float32) ** levels(streams_of[7], (COLUMNS,), ((0, 64),), -0.2, 0.2), 0.5, 1.0)
    return dict(states=states, obs_weights=obs_weights, observations=observations, obs_precision=obs_precision, resample_index=resample_index, blend_weight=blend_weight, stencil_region=stencil_region, stencil_weight=stencil_weight)


def make_tapers(region_width):
    position = jnp.arange(3 * region_width).astype(jnp.float32)
    centred = (position - (3 * region_width - 1) / 2.0) / region_width
    return jnp.exp(-0.5 * centred * centred).reshape(3, region_width)

def region_transforms(rim_blocks, resample_index, blend_weight):
    members = rim_blocks.shape[0] - 1
    region_width = rim_blocks.shape[3]
    region_count = rim_blocks.shape[2] - 2
    tapers = make_tapers(region_width)
    grams = jnp.zeros((region_count, members + 1, members + 1), jnp.float32)
    for offset in range(3):
        window_part = rim_blocks[:, :, offset:offset + region_count, :]
        grams = grams + jnp.einsum('ioak,joak->aij', window_part * tapers[offset], window_part, precision=lax.Precision.HIGHEST)
    cross_gram = grams[:, :members, :members]
    drive_vec = grams[:, :members, members]
    identity_mat = jnp.eye(members, dtype=jnp.float32)
    scaled_gram = identity_mat + cross_gram / (members - 1.0)
    norm_scale = 1.0 + jnp.sqrt(lax.optimization_barrier(jnp.sum(cross_gram * cross_gram, axis=(1, 2)))) / (members - 1.0)
    iterate_y = scaled_gram / norm_scale[:, None, None]
    iterate_z = jnp.broadcast_to(identity_mat, scaled_gram.shape)
    for sweep in range(NS_ITERS):
        factor = 0.5 * (3.0 * identity_mat - jnp.matmul(iterate_z, iterate_y, precision=lax.Precision.HIGHEST))
        iterate_y = jnp.matmul(iterate_y, factor, precision=lax.Precision.HIGHEST)
        iterate_z = jnp.matmul(factor, iterate_z, precision=lax.Precision.HIGHEST)
    inv_root = iterate_z / jnp.sqrt(norm_scale)[:, None, None]
    inv_gram = jnp.matmul(inv_root, inv_root, precision=lax.Precision.HIGHEST)
    mean_weight = jnp.einsum('aij,aj->ai', inv_gram, drive_vec, precision=lax.Precision.HIGHEST) / (members - 1.0)
    weights = mean_weight[:, :, None] + inv_root
    etkf_part = 1.0 / members + weights - lax.optimization_barrier(jnp.mean(weights, axis=1, keepdims=True))
    member_ids = jnp.arange(members, dtype=jnp.int32)
    resampled = (resample_index[:, None, :] == member_ids[None, :, None]).astype(jnp.float32)
    mixed = (1.0 - blend_weight)[:, None, None] * etkf_part + blend_weight[:, None, None] * resampled
    return mixed.astype(jnp.bfloat16)

def reference(states, obs_weights, observations, obs_precision, resample_index, blend_weight, stencil_region, stencil_weight):
    final_state = states[LAGS - 1]
    obs_space = jnp.einsum('ol,mlc->moc', obs_weights.astype(jnp.float32), final_state.astype(jnp.float32), precision=lax.Precision.HIGHEST)
    obs_mean = lax.optimization_barrier(jnp.mean(obs_space, axis=0))
    root_prec = jnp.sqrt(obs_precision)
    obs_perturb = (obs_space - obs_mean) * root_prec
    innovation = (observations - obs_mean) * root_prec
    scaled = jnp.concatenate([obs_perturb, innovation[None]], axis=0)
    extended = jnp.pad(scaled, ((0, 0), (0, 0), (COLS_REG, COLS_REG)))
    rim_blocks = extended.reshape(M + 1, NOBS, REGIONS + 2, COLS_REG)
    transforms = region_transforms(rim_blocks, resample_index, blend_weight).astype(jnp.float32)
    own_region = (jnp.arange(COLUMNS, dtype=jnp.int32) // COLS_REG).astype(jnp.int32)
    column_maps = stencil_weight[:, None, None] * transforms[own_region] + (1.0 - stencil_weight)[:, None, None] * transforms[stencil_region]
    column_maps = column_maps.astype(jnp.bfloat16).astype(jnp.float32)

    def apply_lag(slab):
        return jnp.einsum('jlc,cji->ilc', slab.astype(jnp.float32), column_maps, precision=lax.Precision.HIGHEST).astype(jnp.bfloat16)
    return lax.map(apply_lag, states)
```

```python
import math

import jax
import jax.numpy as jnp
from jax import lax
from jax.experimental import pallas as pl
from jax.experimental.pallas import tpu as pltpu
from jax.sharding import PartitionSpec as P

M = 80
LEV = 127
NOBS = 24
COLS = 128
WIDTH = 8
REG = 16
NS_ITERS = 8
KB = 256
MX = 96
GROUP = 8
F32 = jnp.float32
BF16 = jnp.bfloat16
MESH = pl.DeviceIdType.MESH

TAPER = [
    [math.exp(-0.5 * ((q * WIDTH + k - (3 * WIDTH - 1) / 2.0) / WIDTH) ** 2) for k in range(WIDTH)]
    for q in range(3)
]
PIECES = ((0, 8), (8, 8), (16, 2))


def split(x):
    high = x.astype(BF16)
    return high, (x - high.astype(F32)).astype(BF16)


def halves(x):
    high, low = split(x)
    return jnp.concatenate([high, low], axis=1)


def product(a, b):
    gap = jnp.zeros((128 - M, 256), BF16)
    out = jnp.dot(a, jnp.concatenate([b, gap, b, gap], axis=0), preferred_element_type=F32)
    return out[:, :128] + out[:, 128:]


def pair_rows(value, spread, chosen):
    first = value.astype(BF16)
    rest = value - first.astype(F32)
    second = rest.astype(BF16)
    third = (rest - second.astype(F32)).astype(BF16)
    dims = (((0,), (0,)), ((), ()))
    total = lax.dot_general(first, spread, dims, preferred_element_type=F32)
    total += lax.dot_general(second, spread, dims, preferred_element_type=F32)
    total += lax.dot_general(third, spread, dims, preferred_element_type=F32)
    return jnp.sum(jnp.where(chosen, total, 0.0).reshape(REG, WIDTH, KB), axis=1)


def prepare(w, y, pr, wb, yrow, rrow):
    row = lax.broadcasted_iota(jnp.int32, (NOBS, KB), 0)
    lane = lax.broadcasted_iota(jnp.int32, (NOBS, KB), 1)
    spread = jnp.where((lane % NOBS == row) & (lane < WIDTH * NOBS), 1.0, 0.0).astype(BF16)
    row = lax.broadcasted_iota(jnp.int32, (COLS, KB), 0)
    lane = lax.broadcasted_iota(jnp.int32, (COLS, KB), 1)
    chosen = lane // NOBS == row % WIDTH
    yrow[...] = pair_rows(y[...], spread, chosen)
    rrow[...] = pair_rows(jnp.sqrt(pr[...]), spread, chosen)
    wide = lax.dot_general(w[...], spread, (((0,), (0,)), ((), ())), preferred_element_type=F32)
    wide = jnp.concatenate([wide, jnp.zeros((1, KB), F32)], axis=0)
    for k in range(WIDTH):
        wb[k * 128 : (k + 1) * 128] = jnp.where(lane // NOBS == k, wide, 0.0).astype(BF16)


def scaled_blocks(regions, xc, wb, yrow, rrow):
    rows = []
    for r in regions:
        rows.append(jnp.concatenate([xc[r * WIDTH + k] for k in range(WIDTH)], axis=1))
    out = jnp.dot(jnp.concatenate(rows, axis=0), wb[...], preferred_element_type=F32)
    top = lax.broadcasted_iota(jnp.int32, (MX - M, KB), 0) == 0
    blocks = []
    for k, r in enumerate(regions):
        obs = out[k * M : (k + 1) * M]
        mean = jnp.sum(obs, axis=0, keepdims=True) * (1.0 / M)
        innovation = jnp.where(top, yrow[pl.ds(r, 1), :] - mean, 0.0)
        blocks.append(
            jnp.concatenate([obs - mean, innovation], axis=0) * rrow[pl.ds(r, 1), :]
        )
    return blocks


def gram_parts(x, parts):
    high, low = split(x)
    across = jnp.concatenate([x, jnp.zeros((128 - MX, KB), F32)], axis=0).T
    highs, lows = [], []
    for q in parts:
        tapered = [across[k * NOBS : (k + 1) * NOBS] * TAPER[q][k] for k in range(WIDTH)]
        h, l = split(jnp.concatenate(tapered, axis=0))
        highs.append(h)
        lows.append(l)
    used = WIDTH * NOBS
    n = 128 * len(parts)
    right = jnp.concatenate(highs + lows, axis=1)
    out = jnp.dot(high[:, :used], right, preferred_element_type=F32)
    out2 = jnp.dot(low[:, :used], right[:, :n], preferred_element_type=F32)
    total = out[:, :n] + out[:, n:] + out2
    return [total[:, k * 128 : (k + 1) * 128] for k in range(len(parts))]


def add_block(x, r, gram):
    parts = gram_parts(x, (0, 1, 2))
    gram[r + 2] += parts[0]
    gram[r + 1] += parts[1]
    gram[r] += parts[2]


def transforms_group(first, gram, resample, blend, t, ys, zs):
    row = lax.broadcasted_iota(jnp.int32, (M, 128), 0)
    col = lax.broadcasted_iota(jnp.int32, (M, 128), 1)
    eye = (row == col).astype(F32)
    norms = []
    regions = [lax.rem(first + k + 12, REG) for k in range(GROUP)]
    for k, r in enumerate(regions):
        cross = jnp.where(col < M, gram[r + 1, :M, :], 0.0)
        square = jnp.sum(cross * cross, axis=0, keepdims=True)
        norm = 1.0 + jnp.sqrt(jnp.sum(square, axis=1, keepdims=True)) * (1.0 / (M - 1))
        norms.append(norm)
        y = (eye + cross * (1.0 / (M - 1))) / norm
        e = halves(1.5 * eye - 0.5 * y)
        ys[k] = halves(product(halves(y), e))
        zs[k] = e

    @pl.loop(0, NS_ITERS - 2)
    def _(sweep):
        factors = [
            halves(1.5 * eye - 0.5 * product(zs[k], ys[k])) for k in range(GROUP)
        ]
        for k in range(GROUP):
            both = product(jnp.concatenate([ys[k], zs[k]], axis=0), factors[k])
            ys[k] = halves(both[:M])
            zs[k] = halves(both[M:])

    for k, r in enumerate(regions):
        e = halves(1.5 * eye - 0.5 * product(zs[k], ys[k]))
        root = product(zs[k], e) / jnp.sqrt(norms[k])
        drive = gram[r + 1, :M, M : M + 1]
        half = jnp.sum(root * drive, axis=0, keepdims=True)
        mean_weight = jnp.sum(root * half, axis=1, keepdims=True) * (1.0 / (M - 1))
        weights = mean_weight + root
        etkf = 1.0 / M + weights - jnp.sum(weights, axis=0, keepdims=True) * (1.0 / M)
        drawn = (resample[pl.ds(r, 1), :] == row).astype(F32)
        share = blend[r]
        t[first + k] = ((1.0 - share) * etkf + share * drawn).astype(BF16)


def make_transform_kernel(lags, spaces):
    last = lags - 1

    def kernel(
        st, w, y, pr, resample, blend, t_out, s_out,
        xc, sc, wb, yrow, rrow, edge, halo, gram, t, ys, zs,
        x_send, x_recv, e_send, e_recv, p_next, p_side, p_recv, local,
    ):
        lag = lax.axis_index("lag")
        here = lax.axis_index("space")
        odd = lax.rem(lag, 2)
        has_left, has_right = here > 0, here < spaces - 1
        left, right = here - 1, here + 1
        barrier = pltpu.get_barrier_semaphore()

        def greet(where):
            pl.semaphore_signal(barrier, inc=1, device_id=where, device_id_type=MESH)

        @pl.when(lag == last)
        def _():
            @pl.when(has_left)
            def _():
                greet({"space": left})

            @pl.when(has_right)
            def _():
                greet({"space": right})

        @pl.when(lag < last)
        def _():
            greet({"lag": lag + 1 + odd})

        def columns_first():
            for k in range(0, 128, 16):
                stop = min(k + 16, LEV)
                sc[:, k:stop, :M] = jnp.transpose(st[k:stop], (2, 0, 1))
            pltpu.make_async_copy(sc, s_out, local.at[0]).start()

        def side(p):
            first, count = PIECES[p]
            ref = t.at[pl.ds(first, count)]
            return pltpu.make_async_remote_copy(
                src_ref=ref, dst_ref=ref, send_sem=p_side.at[p], recv_sem=p_recv.at[p],
                device_id={"lag": lag - 1}, device_id_type=MESH)

        def onward(p):
            first, count = PIECES[p]
            ref = t.at[pl.ds(first, count)]
            return pltpu.make_async_remote_copy(
                src_ref=ref, dst_ref=ref, send_sem=p_next.at[p], recv_sem=p_recv.at[p],
                device_id={"lag": lag - 2}, device_id_type=MESH)

        def block_copy(k, where):
            return pltpu.make_async_remote_copy(
                src_ref=edge.at[k], dst_ref=halo.at[1 - k], send_sem=x_send.at[k],
                recv_sem=x_recv.at[1 - k], device_id={"space": where}, device_id_type=MESH)

        def edge_copy(k, where):
            return pltpu.make_async_remote_copy(
                src_ref=t.at[4 if k == 0 else 3], dst_ref=t.at[17 - k], send_sem=e_send.at[k],
                recv_sem=e_recv.at[1 - k], device_id={"space": where}, device_id_type=MESH)

        sides = ((0, has_left, left), (1, has_right, right))

        @pl.when(lag == last)
        def _():
            prepare(w, y, pr, wb, yrow, rrow)
            xc[...] = jnp.transpose(
                jnp.concatenate([st[...], jnp.zeros((1, M, COLS), BF16)], axis=0), (2, 1, 0))

            @pl.loop(0, REG + 2)
            def _(r):
                gram[r] = jnp.zeros((MX, 128), F32)

            ends = scaled_blocks((0, REG - 1), xc, wb, yrow, rrow)
            edge[0], edge[1] = ends
            pl.semaphore_wait(
                barrier, 2 + has_left.astype(jnp.int32) + has_right.astype(jnp.int32))
            for k, there, where in sides:
                @pl.when(there)
                def _(k=k, where=where):
                    block_copy(k, where).start()
            add_block(edge[0], 0, gram)
            add_block(edge[1], REG - 1, gram)

            @pl.loop(0, (REG - 2) // 2)
            def _(i):
                pair = (1 + 2 * i, 2 + 2 * i)
                for r, x in zip(pair, scaled_blocks(pair, xc, wb, yrow, rrow)):
                    add_block(x, r, gram)

            for k, there, where in sides:
                @pl.when(there)
                def _(k=k, where=where):
                    block_copy(1 - k, where).wait_recv()
                    block_copy(k, where).wait_send()

            @pl.when(has_left)
            def _():
                gram[1] += gram_parts(halo[0], (0,))[0]

            @pl.when(has_right)
            def _():
                gram[REG] += gram_parts(halo[1], (2,))[0]

            for p in range(2):
                transforms_group(p * GROUP, gram, resample, blend, t, ys, zs)
                side(p).start()
                onward(p).start()
                if p == 0:
                    for k, there, where in sides:
                        @pl.when(there)
                        def _(k=k, where=where):
                            edge_copy(k, where).start()
            for k, there, where in sides:
                @pl.when(there)
                def _(k=k, where=where):
                    edge_copy(1 - k, where).wait_recv()
                    edge_copy(k, where).wait_send()

                @pl.when(jnp.logical_not(there))
                def _(k=k):
                    t[16 + k] = jnp.zeros((M, 128), BF16)
            side(2).start()
            onward(2).start()
            columns_first()
            for p in range(3):
                side(p).wait_send()
                onward(p).wait_send()

        @pl.when(lag < last)
        def _():
            columns_first()

            @pl.when(odd == 1)
            def _():
                pl.semaphore_wait(barrier, 1 + (lag > 1).astype(jnp.int32))

            for p in range(3):
                side(p).wait_recv()

                @pl.when(odd == 1)
                def _(p=p):
                    side(p).start()

                    @pl.when(lag > 1)
                    def _():
                        onward(p).start()

            @pl.when(odd == 1)
            def _():
                for p in range(3):
                    side(p).wait_send()

                    @pl.when(lag > 1)
                    def _(p=p):
                        onward(p).wait_send()

        out = pltpu.make_async_copy(t, t_out, local.at[1])
        out.start()
        pltpu.make_async_copy(sc, s_out, local.at[0]).wait()
        out.wait()

    return kernel


def transforms_call(lags, spaces, st, w, y, pr, resample, blend):
    vmem = pl.BlockSpec(memory_space=pltpu.VMEM)
    hbm = pl.BlockSpec(memory_space=pl.ANY)
    smem = pl.BlockSpec(memory_space=pltpu.SMEM)
    dma = pltpu.SemaphoreType.DMA
    return pl.pallas_call(
        make_transform_kernel(lags, spaces),
        out_shape=(
            jax.ShapeDtypeStruct((REG + 2, M, 128), BF16),
            jax.ShapeDtypeStruct((COLS, 128, 128), BF16),
        ),
        in_specs=[vmem, vmem, vmem, vmem, vmem, smem],
        out_specs=(hbm, hbm),
        scratch_shapes=[
            pltpu.VMEM((COLS, M, 128), BF16),
            pltpu.VMEM((COLS, 128, 128), BF16),
            pltpu.VMEM((WIDTH * 128, KB), BF16),
            pltpu.VMEM((REG, KB), F32),
            pltpu.VMEM((REG, KB), F32),
            pltpu.VMEM((2, MX, KB), F32),
            pltpu.VMEM((2, MX, KB), F32),
            pltpu.VMEM((REG + 2, MX, 128), F32),
            pltpu.VMEM((REG + 2, M, 128), BF16),
            pltpu.VMEM((GROUP, M, 256), BF16),
            pltpu.VMEM((GROUP, M, 256), BF16),
            dma((2,)), dma((2,)), dma((2,)), dma((2,)), dma((3,)), dma((3,)), dma((3,)), dma((2,)),
        ],
        compiler_params=pltpu.CompilerParams(
            collective_id=0, has_side_effects=True, vmem_limit_bytes=48 * 2**20),
    )(st, w, y, pr, resample, blend)


UNROLL = 16
CHUNKS = 8


def analysis_kernel(s, t, near, weight, out, sv, tf, o, ov, s_sem, o_sem):
    step = COLS // CHUNKS

    def fetch(k):
        return pltpu.make_async_copy(
            s.at[pl.ds(k * step, step)], sv.at[pl.ds(k * step, step)], s_sem.at[k])

    for k in range(CHUNKS):
        fetch(k).start()
    base = lax.axis_index("space") * REG

    @pl.loop(0, REG + 2)
    def _(r):
        tf[r] = t[r].astype(F32)

    def column(c):
        beside = near[c] - base
        slot = jnp.where(beside < 0, REG, jnp.where(beside >= REG, REG + 1, (beside + 4) % REG))
        own = (c // WIDTH + 4) % REG
        share = weight[c]
        maps = (share * tf[own] + (1.0 - share) * tf[slot]).astype(BF16)
        o[c] = jnp.dot(sv[c, :, :M], maps, preferred_element_type=F32).astype(BF16)

    @pl.loop(0, CHUNKS)
    def _(k):
        fetch(k).wait()
        for i in range(step):
            column(k * step + i)

    def store(k):
        first = k * 16
        count = min(16, LEV - first)
        return pltpu.make_async_copy(
            ov.at[pl.ds(first, count)], out.at[pl.ds(first, count)], o_sem.at[k])

    for k in range(8):
        first, stop = k * 16, min(k * 16 + 16, LEV)
        turned = jnp.transpose(o[:, first : first + 16, :M], (1, 2, 0))
        ov[first:stop] = turned[: stop - first]
        store(k).start()
    for k in range(8):
        store(k).wait()


def analysis_call(s, t, near, weight):
    vmem = pl.BlockSpec(memory_space=pltpu.VMEM)
    hbm = pl.BlockSpec(memory_space=pl.ANY)
    smem = pl.BlockSpec(memory_space=pltpu.SMEM)
    return pl.pallas_call(
        analysis_kernel,
        out_shape=jax.ShapeDtypeStruct((LEV, M, COLS), BF16),
        in_specs=[hbm, vmem, smem, smem],
        out_specs=hbm,
        scratch_shapes=[
            pltpu.VMEM((COLS, 128, 128), BF16),
            pltpu.VMEM((REG + 2, M, 128), F32),
            pltpu.VMEM((COLS, 128, 128), BF16),
            pltpu.VMEM((LEV, M, COLS), BF16),
            pltpu.SemaphoreType.DMA((CHUNKS,)),
            pltpu.SemaphoreType.DMA((8,)),
        ],
        compiler_params=pltpu.CompilerParams(vmem_limit_bytes=48 * 2**20),
    )(s, t, near, weight)


def per_device(
    states, obs_weights, observations, obs_precision, resample_index, blend_weight,
    stencil_region, stencil_weight,
):
    st = jnp.transpose(states[0], (1, 0, 2))
    resample = jnp.pad(resample_index, ((0, 0), (0, 128 - M)), constant_values=-1)
    t, s = transforms_call(
        lax.axis_size("lag"), lax.axis_size("space"),
        st, obs_weights, observations, obs_precision, resample, blend_weight)
    out = analysis_call(s, t, stencil_region, stencil_weight)
    return jnp.transpose(out, (1, 0, 2))[None]


def solution(mesh):
    in_specs = (
        P("lag", None, None, "space"), P(), P(None, "space"), P(None, "space"),
        P("space", None), P("space"), P("space"), P("space"),
    )
    return jax.shard_map(
        per_device, mesh=mesh, in_specs=in_specs, out_specs=P("lag", None, None, "space"),
        check_vma=False)
```

```python
import math

import jax
import jax.numpy as jnp
from jax import lax
from jax.experimental import pallas as pl
from jax.experimental.pallas import tpu as pltpu
from jax.sharding import PartitionSpec as P

M = 80
LEV = 127
NOBS = 24
COLS = 128
WIDTH = 8
REG = 16
NS_ITERS = 8
KB = 256
MX = 96
UNROLL = 16
F32 = jnp.float32
BF16 = jnp.bfloat16
MESH = pl.DeviceIdType.MESH

TAPER = [
    [math.exp(-0.5 * ((q * WIDTH + k - (3 * WIDTH - 1) / 2.0) / WIDTH) ** 2) for k in range(WIDTH)]
    for q in range(3)
]


def split(x):
    high = x.astype(BF16)
    return high, (x - high.astype(F32)).astype(BF16)


def halves(x):
    high, low = split(x)
    return jnp.concatenate([high, low], axis=1)


def product(a, b):
    gap = jnp.zeros((128 - M, 256), BF16)
    out = jnp.dot(a, jnp.concatenate([b, gap, b, gap], axis=0), preferred_element_type=F32)
    return out[:, :128] + out[:, 128:]


def pair_rows(value, spread, chosen):
    first = value.astype(BF16)
    rest = value - first.astype(F32)
    second = rest.astype(BF16)
    third = (rest - second.astype(F32)).astype(BF16)
    dims = (((0,), (0,)), ((), ()))
    total = lax.dot_general(first, spread, dims, preferred_element_type=F32)
    total += lax.dot_general(second, spread, dims, preferred_element_type=F32)
    total += lax.dot_general(third, spread, dims, preferred_element_type=F32)
    return jnp.sum(jnp.where(chosen, total, 0.0).reshape(REG, WIDTH, KB), axis=1)


def prepare(w, y, pr, wb, yrow, rrow):
    row = lax.broadcasted_iota(jnp.int32, (NOBS, KB), 0)
    lane = lax.broadcasted_iota(jnp.int32, (NOBS, KB), 1)
    spread = jnp.where((lane % NOBS == row) & (lane < WIDTH * NOBS), 1.0, 0.0).astype(BF16)
    row = lax.broadcasted_iota(jnp.int32, (COLS, KB), 0)
    lane = lax.broadcasted_iota(jnp.int32, (COLS, KB), 1)
    chosen = lane // NOBS == row % WIDTH
    yrow[...] = pair_rows(y[...], spread, chosen)
    rrow[...] = pair_rows(jnp.sqrt(pr[...]), spread, chosen)
    wide = lax.dot_general(w[...], spread, (((0,), (0,)), ((), ())), preferred_element_type=F32)
    wide = jnp.concatenate([wide, jnp.zeros((1, KB), F32)], axis=0)
    for k in range(WIDTH):
        wb[k * 128 : (k + 1) * 128] = jnp.where(lane // NOBS == k, wide, 0.0).astype(BF16)


def scaled_blocks(regions, xc, wb, yrow, rrow):
    rows = []
    for r in regions:
        rows.append(jnp.concatenate([xc[r * WIDTH + k] for k in range(WIDTH)], axis=1))
    out = jnp.dot(jnp.concatenate(rows, axis=0), wb[...], preferred_element_type=F32)
    top = lax.broadcasted_iota(jnp.int32, (MX - M, KB), 0) == 0
    blocks = []
    for k, r in enumerate(regions):
        obs = out[k * M : (k + 1) * M]
        mean = jnp.sum(obs, axis=0, keepdims=True) * (1.0 / M)
        innovation = jnp.where(top, yrow[pl.ds(r, 1), :] - mean, 0.0)
        blocks.append(
            jnp.concatenate([obs - mean, innovation], axis=0) * rrow[pl.ds(r, 1), :]
        )
    return blocks


def gram_parts(x, parts):
    high, low = split(x)
    across = jnp.concatenate([x, jnp.zeros((128 - MX, KB), F32)], axis=0).T
    highs, lows = [], []
    for q in parts:
        tapered = [across[k * NOBS : (k + 1) * NOBS] * TAPER[q][k] for k in range(WIDTH)]
        h, l = split(jnp.concatenate(tapered, axis=0))
        highs.append(h)
        lows.append(l)
    used = WIDTH * NOBS
    n = 128 * len(parts)
    right = jnp.concatenate(highs + lows, axis=1)
    out = jnp.dot(high[:, :used], right, preferred_element_type=F32)
    out2 = jnp.dot(low[:, :used], right[:, :n], preferred_element_type=F32)
    total = out[:, :n] + out[:, n:] + out2
    return [total[:, k * 128 : (k + 1) * 128] for k in range(len(parts))]


def add_block(x, r, gram):
    parts = gram_parts(x, (0, 1, 2))
    gram[r + 2] += parts[0]
    gram[r + 1] += parts[1]
    gram[r] += parts[2]


def transforms_group(items, gram, ys, zs):
    row = lax.broadcasted_iota(jnp.int32, (M, 128), 0)
    col = lax.broadcasted_iota(jnp.int32, (M, 128), 1)
    eye = (row == col).astype(F32)
    count = len(items)
    norms = []
    for k, (slot, _, _) in enumerate(items):
        cross = jnp.where(col < M, gram[slot, :M, :], 0.0)
        square = jnp.sum(cross * cross, axis=0, keepdims=True)
        norm = 1.0 + jnp.sqrt(jnp.sum(square, axis=1, keepdims=True)) * (1.0 / (M - 1))
        norms.append(norm)
        y = (eye + cross * (1.0 / (M - 1))) / norm
        e = halves(1.5 * eye - 0.5 * y)
        ys[k] = halves(product(halves(y), e))
        zs[k] = e

    @pl.loop(0, NS_ITERS - 2)
    def _(sweep):
        factors = [halves(1.5 * eye - 0.5 * product(zs[k], ys[k])) for k in range(count)]
        for k in range(count):
            both = product(jnp.concatenate([ys[k], zs[k]], axis=0), factors[k])
            ys[k] = halves(both[:M])
            zs[k] = halves(both[M:])

    result = []
    for k, (slot, drawn_row, share) in enumerate(items):
        e = halves(1.5 * eye - 0.5 * product(zs[k], ys[k]))
        root = product(zs[k], e) / jnp.sqrt(norms[k])
        drive = gram[slot, :M, M : M + 1]
        half = jnp.sum(root * drive, axis=0, keepdims=True)
        mean_weight = jnp.sum(root * half, axis=1, keepdims=True) * (1.0 / (M - 1))
        weights = mean_weight + root
        etkf = 1.0 / M + weights - jnp.sum(weights, axis=0, keepdims=True) * (1.0 / M)
        drawn = (drawn_row == row).astype(F32)
        result.append((1.0 - share) * etkf + share * drawn)
    return result


def pack(maps):
    lane = lax.broadcasted_iota(jnp.int32, (M, 128), 1)
    a, b, c, d, e, f, g, h = maps

    def tail(first, second=None, cut=128):
        return first if second is None else jnp.where(lane < cut, first, second)

    spare = (
        pltpu.roll(f, 80, 1),
        tail(pltpu.roll(f, 32, 1), pltpu.roll(g, 112, 1), 112),
        pltpu.roll(g, 64, 1),
        tail(pltpu.roll(g, 16, 1), pltpu.roll(h, 96, 1), 96),
        pltpu.roll(h, 48, 1),
    )
    return [
        jnp.where(lane < M, kept, extra).astype(BF16)
        for kept, extra in zip((a, b, c, d, e), spare)
    ]


def unpack(slabs):
    lane = lax.broadcasted_iota(jnp.int32, (M, 128), 1)
    a, b, c, d, e = slabs
    f = jnp.where(lane < 48, pltpu.roll(a, 48, 1), pltpu.roll(b, 96, 1))
    g = jnp.where(
        lane < 16, pltpu.roll(b, 16, 1),
        jnp.where(lane < 64, pltpu.roll(c, 64, 1), pltpu.roll(d, 112, 1)))
    h = jnp.where(lane < 32, pltpu.roll(d, 32, 1), pltpu.roll(e, 80, 1))
    return [a, b, c, d, e, f, g, h]


ODD_REGIONS = (12, 13, 14, 15, 0, 1, 2, 3, -1, 16)
EVEN_REGIONS = (4, 5, 6, 7, 8, 9, 10, 11)
SLABS = 12
ODD_PIECES = ((0, 2), (2, 2), (4, 3))
EVEN_PIECES = ((7, 2), (9, 2), (11, 1))
LEVEL_CHUNKS = ((0, 32), (32, 32), (64, 32), (96, 31))


def make_transform_kernel(lags, spaces):
    last = lags - 1

    def kernel(
        st_hbm, w_hbm, y_hbm, pr_hbm, resample_hbm, blend_hbm, t_out, sc,
        st, w, y, pr, resample, blend,
        xc, wb, yrow, rrow, edge, halo, gram, t, ys, zs,
        in_sem, st_sem, x_send, x_recv, g_send, g_recv,
        p_next, p_side, own_recv, other_recv, ready,
    ):
        lag = lax.axis_index("lag")
        here = lax.axis_index("space")
        odd = lax.rem(lag, 2)
        sibling = lag + 1 - 2 * odd
        has_left, has_right = here > 0, here < spaces - 1
        left, right = here - 1, here + 1
        barrier = pltpu.get_barrier_semaphore()
        is_last = lag == last

        def greet(where):
            pl.semaphore_signal(barrier, inc=1, device_id=where, device_id_type=MESH)

        greet({"lag": sibling})

        @pl.when(lag >= 2)
        def _():
            greet({"lag": lag - 2})

        @pl.when(is_last)
        def _():
            @pl.when(has_left)
            def _():
                greet({"space": left})

            @pl.when(has_right)
            def _():
                greet({"space": right})

        def level_copy(k):
            first, count = LEVEL_CHUNKS[k]
            return pltpu.make_async_copy(
                st_hbm.at[pl.ds(first, count)], st.at[pl.ds(first, count)], st_sem.at[k])

        small = [
            pltpu.make_async_copy(src, dst, in_sem.at[k])
            for k, (src, dst) in enumerate(
                ((w_hbm, w), (y_hbm, y), (pr_hbm, pr), (resample_hbm, resample), (blend_hbm, blend)))
        ]
        for copy in small:
            copy.start()
        for k in range(len(LEVEL_CHUNKS)):
            level_copy(k).start()
        for copy in small:
            copy.wait()

        def columns_first():
            for k in range(0, 128, 16):
                stop = min(k + 16, LEV)
                sc[:, k:stop, :M] = jnp.transpose(st[k:stop], (2, 0, 1))

        def side(k, pieces):
            ref = t.at[pl.ds(*pieces[k])]
            return pltpu.make_async_remote_copy(
                src_ref=ref, dst_ref=ref, send_sem=p_side.at[k], recv_sem=other_recv.at[k],
                device_id={"lag": sibling}, device_id_type=MESH)

        def onward(k, pieces):
            ref = t.at[pl.ds(*pieces[k])]
            return pltpu.make_async_remote_copy(
                src_ref=ref, dst_ref=ref, send_sem=p_next.at[k], recv_sem=own_recv.at[k],
                device_id={"lag": lag - 2}, device_id_type=MESH)

        def block_copy(k, where):
            return pltpu.make_async_remote_copy(
                src_ref=edge.at[k], dst_ref=halo.at[1 - k], send_sem=x_send.at[k],
                recv_sem=x_recv.at[1 - k], device_id={"space": where}, device_id_type=MESH)

        def gram_copy():
            ref = gram.at[pl.ds(5, 8)]
            return pltpu.make_async_remote_copy(
                src_ref=ref, dst_ref=ref, send_sem=g_send, recv_sem=g_recv,
                device_id={"lag": sibling}, device_id_type=MESH)

        def drawn_row(r):
            return resample[r : r + 1, :]

        def wide_row(r):
            return jnp.concatenate([drawn_row(r), jnp.full((1, 48), -1, jnp.int32)], axis=1)

        def item(r):
            return (r + 1, wide_row(r), blend[r])

        def with_extras(x, r):
            values = jnp.concatenate(
                [drawn_row(r).astype(F32), jnp.zeros((1, KB - M), F32)], axis=1)
            which = lax.broadcasted_iota(jnp.int32, (MX, KB), 0)
            return jnp.where(which == M + 1, values, jnp.where(which == M + 2, blend[r], x))

        def outside_item(k, slot):
            drawn = halo[k, 0, M + 1 : M + 2, :128].astype(jnp.int32)
            return (slot, drawn, halo[k, 0, M + 2 : M + 3, :128])

        sides = ((0, has_left, left), (1, has_right, right))

        @pl.when(is_last)
        def _():
            prepare(w, y, pr, wb, yrow, rrow)

            @pl.loop(0, REG + 2)
            def _(r):
                gram[r] = jnp.zeros((MX, 128), F32)

            for k in range(len(LEVEL_CHUNKS)):
                level_copy(k).wait()
            xc[...] = jnp.transpose(
                jnp.concatenate([st[...], jnp.zeros((1, M, COLS), BF16)], axis=0), (2, 1, 0))

            ends = scaled_blocks((0, 1, REG - 1, REG - 2), xc, wb, yrow, rrow)
            edge[0, 0], edge[0, 1] = with_extras(ends[0], 0), ends[1]
            edge[1, 0], edge[1, 1] = with_extras(ends[2], REG - 1), ends[3]
            pl.semaphore_wait(
                barrier, 1 + has_left.astype(jnp.int32) + has_right.astype(jnp.int32))
            for k, there, where in sides:
                @pl.when(there)
                def _(k=k, where=where):
                    block_copy(k, where).start()

            @pl.loop(0, 5)
            def _(i):
                pair = (3 + 2 * i, 4 + 2 * i)
                for r, x in zip(pair, scaled_blocks(pair, xc, wb, yrow, rrow)):
                    add_block(x, r, gram)

            gram_copy().start()
            for r, x in zip((2, 13), scaled_blocks((2, 13), xc, wb, yrow, rrow)):
                add_block(x, r, gram)
            for k, j, r in ((0, 0, 0), (0, 1, 1), (1, 0, REG - 1), (1, 1, REG - 2)):
                add_block(edge[k, j], r, gram)

            for k, there, where in sides:
                @pl.when(there)
                def _(k=k, where=where):
                    block_copy(1 - k, where).wait_recv()
                    block_copy(k, where).wait_send()

                @pl.when(jnp.logical_not(there))
                def _(k=k):
                    halo[k] = jnp.zeros((2, MX, KB), F32)
            near = gram_parts(halo[0, 0], (0, 1))
            gram[1] += near[0]
            gram[0] += near[1] + gram_parts(halo[0, 1], (0,))[0]
            near = gram_parts(halo[1, 0], (1, 2))
            gram[REG] += near[1]
            gram[REG + 1] += near[0] + gram_parts(halo[1, 1], (2,))[0]

            items = [item(r) for r in ODD_REGIONS[:8]]
            items += [outside_item(0, 0), outside_item(1, REG + 1)]
            maps = transforms_group(items, gram, ys, zs)
            for k, slab in enumerate(pack(maps[:8]) + [m.astype(BF16) for m in maps[8:]]):
                t[k] = slab
            gram_copy().wait_send()

        @pl.when(jnp.logical_not(is_last))
        def _():
            for k in range(len(LEVEL_CHUNKS)):
                level_copy(k).wait()
            columns_first()
            pl.semaphore_wait(barrier, 1 + (lag < last - 1).astype(jnp.int32))

            @pl.when(lag < last - 1)
            def _():
                pl.semaphore_signal(
                    ready, inc=1, device_id={"lag": lag + 2}, device_id_type=MESH)

        @pl.when(lag == last - 1)
        def _():
            gram_copy().wait_recv()
            maps = transforms_group([item(r) for r in EVEN_REGIONS], gram, ys, zs)
            for k, slab in enumerate(pack(maps)):
                t[7 + k] = slab

        @pl.when(lag >= 2)
        def _():
            pl.semaphore_wait(ready, 1)

        for parity, own, other in ((1, ODD_PIECES, EVEN_PIECES), (0, EVEN_PIECES, ODD_PIECES)):
            @pl.when(odd == parity)
            def _(own=own, other=other):
                for k in range(3):
                    @pl.when(lag < last - 1)
                    def _(k=k):
                        onward(k, own).wait_recv()

                    side(k, own).start()

                    @pl.when(lag >= 2)
                    def _(k=k):
                        onward(k, own).start()

                @pl.when(is_last)
                def _():
                    columns_first()

                for k in range(3):
                    side(k, other).wait_recv()
                for k in range(3):
                    side(k, own).wait_send()

                    @pl.when(lag >= 2)
                    def _(k=k):
                        onward(k, own).wait_send()

        t_out[...] = t[...]

    return kernel


def transforms_call(lags, spaces, st, w, y, pr, resample, blend):
    vmem = pl.BlockSpec(memory_space=pltpu.VMEM)
    hbm = pl.BlockSpec(memory_space=pltpu.HBM)
    dma = pltpu.SemaphoreType.DMA
    return pl.pallas_call(
        make_transform_kernel(lags, spaces),
        out_shape=(
            jax.ShapeDtypeStruct((SLABS, M, 128), BF16),
            jax.ShapeDtypeStruct((COLS, 128, 128), BF16),
        ),
        in_specs=[hbm] * 6,
        out_specs=(vmem, vmem),
        scratch_shapes=[
            pltpu.VMEM((LEV, M, COLS), BF16),
            pltpu.VMEM((NOBS, LEV), BF16),
            pltpu.VMEM((NOBS, COLS), F32),
            pltpu.VMEM((NOBS, COLS), F32),
            pltpu.VMEM((REG, M), jnp.int32),
            pltpu.SMEM((REG,), F32),
            pltpu.VMEM((COLS, M, 128), BF16),
            pltpu.VMEM((WIDTH * 128, KB), BF16),
            pltpu.VMEM((REG, KB), F32),
            pltpu.VMEM((REG, KB), F32),
            pltpu.VMEM((2, 2, MX, KB), F32),
            pltpu.VMEM((2, 2, MX, KB), F32),
            pltpu.VMEM((REG + 2, MX, 128), F32),
            pltpu.VMEM((SLABS, M, 128), BF16),
            pltpu.VMEM((10, M, 256), BF16),
            pltpu.VMEM((10, M, 256), BF16),
            dma((5,)), dma((4,)), dma((2,)), dma((2,)), dma, dma,
            dma((3,)), dma((3,)), dma((3,)), dma((3,)), pltpu.SemaphoreType.REGULAR,
        ],
        compiler_params=pltpu.CompilerParams(
            collective_id=0, has_side_effects=True, vmem_limit_bytes=24 * 2**20),
    )(*(pltpu.with_memory_space_constraint(x, pltpu.HBM) for x in (st, w, y, pr, resample, blend)))


def analysis_kernel(s, t, near, weight, out, tf, o, ov, o_sem):
    base = lax.axis_index("space") * REG - 1
    slabs = [t[k].astype(F32) for k in range(SLABS)]
    maps = unpack(slabs[:5]) + slabs[5:7] + unpack(slabs[7:])
    for r, m in zip(ODD_REGIONS + EVEN_REGIONS, maps):
        tf[r + 1] = m

    def column(c):
        share = weight[c]
        maps = (share * tf[c // WIDTH + 1] + (1.0 - share) * tf[near[c] - base]).astype(BF16)
        o[c] = jnp.dot(s[c, :, :M], maps, preferred_element_type=F32).astype(BF16)

    @pl.loop(0, COLS, step=UNROLL)
    def _(first):
        for i in range(UNROLL):
            column(first + i)

    def store(k):
        first = k * 16
        count = min(16, LEV - first)
        return pltpu.make_async_copy(
            ov.at[pl.ds(first, count)], out.at[pl.ds(first, count)], o_sem.at[k])

    for k in range(8):
        first, stop = k * 16, min(k * 16 + 16, LEV)
        turned = jnp.transpose(o[:, first : first + 16, :M], (1, 2, 0))
        ov[first:stop] = turned[: stop - first]
        store(k).start()
    for k in range(8):
        store(k).wait()


def analysis_call(s, t, near, weight):
    vmem = pl.BlockSpec(memory_space=pltpu.VMEM)
    hbm = pl.BlockSpec(memory_space=pltpu.HBM)
    smem = pl.BlockSpec(memory_space=pltpu.SMEM)
    return pl.pallas_call(
        analysis_kernel,
        out_shape=jax.ShapeDtypeStruct((LEV, M, COLS), BF16),
        in_specs=[vmem, vmem, smem, smem],
        out_specs=hbm,
        scratch_shapes=[
            pltpu.VMEM((REG + 2, M, 128), F32),
            pltpu.VMEM((COLS, 128, 128), BF16),
            pltpu.VMEM((LEV, M, COLS), BF16),
            pltpu.SemaphoreType.DMA((8,)),
        ],
        compiler_params=pltpu.CompilerParams(vmem_limit_bytes=24 * 2**20),
    )(s, t, near, weight)


def per_device(
    states, obs_weights, observations, obs_precision, resample_index, blend_weight,
    stencil_region, stencil_weight,
):
    st = jnp.transpose(states[0], (1, 0, 2))
    t, s = transforms_call(
        lax.axis_size("lag"), lax.axis_size("space"),
        st, obs_weights, observations, obs_precision, resample_index, blend_weight)
    out = analysis_call(s, t, stencil_region, stencil_weight)
    return jnp.transpose(out, (1, 0, 2))[None]


def solution(mesh):
    in_specs = (
        P("lag", None, None, "space"), P(), P(None, "space"), P(None, "space"),
        P("space", None), P("space"), P("space"), P("space"),
    )
    return jax.shard_map(
        per_device, mesh=mesh, in_specs=in_specs, out_specs=P("lag", None, None, "space"),
        check_vma=False)
```

```python
import math

import jax
import jax.numpy as jnp
from jax import lax
from jax.experimental import pallas as pl
from jax.experimental.pallas import tpu as pltpu
from jax.sharding import PartitionSpec as P

M = 80
LEV = 127
NOBS = 24
COLS = 128
WIDTH = 8
REG = 16
NS_ITERS = 8
KB = 256
MX = 96
F32 = jnp.float32
BF16 = jnp.bfloat16
MESH = pl.DeviceIdType.MESH

TAPER = [
    [math.exp(-0.5 * ((q * WIDTH + k - (3 * WIDTH - 1) / 2.0) / WIDTH) ** 2) for k in range(WIDTH)]
    for q in range(3)
]


def split(x):
    high = x.astype(BF16)
    return high, (x - high.astype(F32)).astype(BF16)


def halves(x):
    high, low = split(x)
    return jnp.concatenate([high, low], axis=1)


def product(a, b):
    gap = jnp.zeros((128 - M, 256), BF16)
    out = jnp.dot(a, jnp.concatenate([b, gap, b, gap], axis=0), preferred_element_type=F32)
    return out[:, :128] + out[:, 128:]


def pair_rows(value, spread, chosen):
    first = value.astype(BF16)
    rest = value - first.astype(F32)
    second = rest.astype(BF16)
    third = (rest - second.astype(F32)).astype(BF16)
    dims = (((0,), (0,)), ((), ()))
    total = lax.dot_general(first, spread, dims, preferred_element_type=F32)
    total += lax.dot_general(second, spread, dims, preferred_element_type=F32)
    total += lax.dot_general(third, spread, dims, preferred_element_type=F32)
    return jnp.sum(jnp.where(chosen, total, 0.0).reshape(REG, WIDTH, KB), axis=1)


def prepare(w, y, pr, wb, yrow, rrow):
    row = lax.broadcasted_iota(jnp.int32, (NOBS, KB), 0)
    lane = lax.broadcasted_iota(jnp.int32, (NOBS, KB), 1)
    spread = jnp.where((lane % NOBS == row) & (lane < WIDTH * NOBS), 1.0, 0.0).astype(BF16)
    row = lax.broadcasted_iota(jnp.int32, (COLS, KB), 0)
    lane = lax.broadcasted_iota(jnp.int32, (COLS, KB), 1)
    chosen = lane // NOBS == row % WIDTH
    yrow[...] = pair_rows(y[...], spread, chosen)
    rrow[...] = pair_rows(jnp.sqrt(pr[...]), spread, chosen)
    wide = lax.dot_general(w[...], spread, (((0,), (0,)), ((), ())), preferred_element_type=F32)
    wide = jnp.concatenate([wide, jnp.zeros((1, KB), F32)], axis=0)
    for k in range(WIDTH):
        wb[k * 128 : (k + 1) * 128] = jnp.where(lane // NOBS == k, wide, 0.0).astype(BF16)


def scaled_blocks(regions, sc, wb, yrow, rrow):
    rows = []
    for r in regions:
        turned = jnp.transpose(sc[pl.ds(r * WIDTH, WIDTH)], (0, 2, 1))[:, :M]
        rows.append(jnp.concatenate([turned[k] for k in range(WIDTH)], axis=1))
    out = jnp.dot(jnp.concatenate(rows, axis=0), wb[...], preferred_element_type=F32)
    top = lax.broadcasted_iota(jnp.int32, (MX - M, KB), 0) == 0
    blocks = []
    for k, r in enumerate(regions):
        obs = out[k * M : (k + 1) * M]
        mean = jnp.sum(obs, axis=0, keepdims=True) * (1.0 / M)
        innovation = jnp.where(top, yrow[pl.ds(r, 1), :] - mean, 0.0)
        blocks.append(
            jnp.concatenate([obs - mean, innovation], axis=0) * rrow[pl.ds(r, 1), :]
        )
    return blocks


def block_terms(x, parts):
    left = split(x)
    across = jnp.concatenate([x, jnp.zeros((128 - MX, KB), F32)], axis=0).T
    gap = jnp.zeros((KB - WIDTH * NOBS, 128), F32)
    terms = {}
    for q in parts:
        tapered = [across[k * NOBS : (k + 1) * NOBS] * TAPER[q][k] for k in range(WIDTH)]
        terms[q] = (*left, halves(jnp.concatenate(tapered + [gap], axis=0)))
    return terms


def gram_of(terms):
    high, low, right = zip(*terms)
    right = jnp.concatenate(right, axis=0)
    out = jnp.dot(jnp.concatenate(high, axis=1), right, preferred_element_type=F32)
    out2 = jnp.dot(jnp.concatenate(low, axis=1), right[:, :128], preferred_element_type=F32)
    return out[:, :128] + out[:, 128:] + out2


def region_gram(r, blocks):
    return gram_of([blocks[r - 1 + q][q] for q in range(3)])


def transforms_group(items, gram, ys, zs):
    row = lax.broadcasted_iota(jnp.int32, (M, 128), 0)
    col = lax.broadcasted_iota(jnp.int32, (M, 128), 1)
    eye = (row == col).astype(F32)
    count = len(items)
    norms = []
    for k, (slot, _, _) in enumerate(items):
        cross = jnp.where(col < M, gram[slot, :M, :], 0.0)
        square = jnp.sum(cross * cross, axis=0, keepdims=True)
        norm = 1.0 + jnp.sqrt(jnp.sum(square, axis=1, keepdims=True)) * (1.0 / (M - 1))
        norms.append(norm)
        y = (eye + cross * (1.0 / (M - 1))) / norm
        e = halves(1.5 * eye - 0.5 * y)
        ys[k] = halves(product(halves(y), e))
        zs[k] = e

    @pl.loop(0, NS_ITERS - 2)
    def _(sweep):
        factors = [halves(1.5 * eye - 0.5 * product(zs[k], ys[k])) for k in range(count)]
        for k in range(count):
            both = product(jnp.concatenate([ys[k], zs[k]], axis=0), factors[k])
            ys[k] = halves(both[:M])
            zs[k] = halves(both[M:])

    result = []
    for k, (slot, drawn_row, share) in enumerate(items):
        e = halves(1.5 * eye - 0.5 * product(zs[k], ys[k]))
        root = product(zs[k], e) / jnp.sqrt(norms[k])
        drive = gram[slot, :M, M : M + 1]
        half = jnp.sum(root * drive, axis=0, keepdims=True)
        mean_weight = jnp.sum(root * half, axis=1, keepdims=True) * (1.0 / (M - 1))
        weights = mean_weight + root
        etkf = 1.0 / M + weights - jnp.sum(weights, axis=0, keepdims=True) * (1.0 / M)
        drawn = (drawn_row == row).astype(F32)
        result.append((1.0 - share) * etkf + share * drawn)
    return result


def pack(maps):
    lane = lax.broadcasted_iota(jnp.int32, (M, 128), 1)
    a, b, c, d, e, f, g, h = maps

    def tail(first, second=None, cut=128):
        return first if second is None else jnp.where(lane < cut, first, second)

    spare = (
        pltpu.roll(f, 80, 1),
        tail(pltpu.roll(f, 32, 1), pltpu.roll(g, 112, 1), 112),
        pltpu.roll(g, 64, 1),
        tail(pltpu.roll(g, 16, 1), pltpu.roll(h, 96, 1), 96),
        pltpu.roll(h, 48, 1),
    )
    return [
        jnp.where(lane < M, kept, extra).astype(BF16)
        for kept, extra in zip((a, b, c, d, e), spare)
    ]


def unpack(slabs):
    lane = lax.broadcasted_iota(jnp.int32, (M, 128), 1)
    a, b, c, d, e = slabs
    f = jnp.where(lane < 48, pltpu.roll(a, 48, 1), pltpu.roll(b, 96, 1))
    g = jnp.where(
        lane < 16, pltpu.roll(b, 16, 1),
        jnp.where(lane < 64, pltpu.roll(c, 64, 1), pltpu.roll(d, 112, 1)))
    h = jnp.where(lane < 32, pltpu.roll(d, 32, 1), pltpu.roll(e, 80, 1))
    return [a, b, c, d, e, f, g, h]


ODD_REGIONS = (12, 13, 14, 15, 0, 1, 2, 3, -1, 16)
EVEN_REGIONS = (4, 5, 6, 7, 8, 9, 10, 11)
SLABS = 12
ODD_PIECES = ((0, 2), (2, 2), (4, 3))
EVEN_PIECES = ((7, 2), (9, 2), (11, 1))
LEVEL_CHUNKS = ((0, 32), (32, 32), (64, 32), (96, 31))


def make_transform_kernel(lags, spaces):
    last = lags - 1

    def kernel(
        st_hbm, w_hbm, y_hbm, pr_hbm, resample_hbm, blend_hbm, t_out, sc,
        st, w, y, pr, resample, blend,
        wb, yrow, rrow, edge, halo, gram, t, ys, zs,
        in_sem, st_sem, x_send, x_recv, g_send, g_recv,
        p_next, p_side, own_recv, other_recv, ready,
    ):
        lag = lax.axis_index("lag")
        here = lax.axis_index("space")
        odd = lax.rem(lag, 2)
        sibling = lag + 1 - 2 * odd
        has_left, has_right = here > 0, here < spaces - 1
        left, right = here - 1, here + 1
        barrier = pltpu.get_barrier_semaphore()
        is_last = lag == last

        def greet(where):
            pl.semaphore_signal(barrier, inc=1, device_id=where, device_id_type=MESH)

        greet({"lag": sibling})

        @pl.when(lag >= 2)
        def _():
            greet({"lag": lag - 2})

        @pl.when(is_last)
        def _():
            @pl.when(has_left)
            def _():
                greet({"space": left})

            @pl.when(has_right)
            def _():
                greet({"space": right})

        def level_copy(k):
            first, count = LEVEL_CHUNKS[k]
            return pltpu.make_async_copy(
                st_hbm.at[pl.ds(first, count)], st.at[pl.ds(first, count)], st_sem.at[k])

        small = [
            pltpu.make_async_copy(src, dst, in_sem.at[k])
            for k, (src, dst) in enumerate(
                ((w_hbm, w), (y_hbm, y), (pr_hbm, pr), (resample_hbm, resample), (blend_hbm, blend)))
        ]
        for copy in small:
            copy.start()
        for k in range(len(LEVEL_CHUNKS)):
            level_copy(k).start()
        for copy in small:
            copy.wait()

        def columns_first():
            gap = jnp.zeros((1, M, COLS), BF16)
            for k, (first, count) in enumerate(LEVEL_CHUNKS):
                level_copy(k).wait()
                for j in range(first, first + count, 16):
                    part = st[j : min(j + 16, LEV)]
                    if j + 16 > LEV:
                        part = jnp.concatenate([part, gap], axis=0)
                    sc[:, j : j + 16, :M] = jnp.transpose(part, (2, 0, 1))

        def side(k, pieces):
            ref = t.at[pl.ds(*pieces[k])]
            return pltpu.make_async_remote_copy(
                src_ref=ref, dst_ref=ref, send_sem=p_side.at[k], recv_sem=other_recv.at[k],
                device_id={"lag": sibling}, device_id_type=MESH)

        def onward(k, pieces):
            ref = t.at[pl.ds(*pieces[k])]
            return pltpu.make_async_remote_copy(
                src_ref=ref, dst_ref=ref, send_sem=p_next.at[k], recv_sem=own_recv.at[k],
                device_id={"lag": lag - 2}, device_id_type=MESH)

        def block_copy(k, where):
            return pltpu.make_async_remote_copy(
                src_ref=edge.at[k], dst_ref=halo.at[1 - k], send_sem=x_send.at[k],
                recv_sem=x_recv.at[1 - k], device_id={"space": where}, device_id_type=MESH)

        def gram_copy():
            ref = gram.at[pl.ds(5, 8)]
            return pltpu.make_async_remote_copy(
                src_ref=ref, dst_ref=ref, send_sem=g_send, recv_sem=g_recv,
                device_id={"lag": sibling}, device_id_type=MESH)

        def drawn_row(r):
            return resample[r : r + 1, :]

        def wide_row(r):
            return jnp.concatenate([drawn_row(r), jnp.full((1, 48), -1, jnp.int32)], axis=1)

        def item(r):
            return (r + 1, wide_row(r), blend[r])

        def with_extras(x, r):
            values = jnp.concatenate(
                [drawn_row(r).astype(F32), jnp.zeros((1, KB - M), F32)], axis=1)
            which = lax.broadcasted_iota(jnp.int32, (MX, KB), 0)
            return jnp.where(which == M + 1, values, jnp.where(which == M + 2, blend[r], x))

        def outside_item(k, slot):
            drawn = halo[k, 0, M + 1 : M + 2, :128].astype(jnp.int32)
            return (slot, drawn, halo[k, 0, M + 2 : M + 3, :128])

        sides = ((0, has_left, left), (1, has_right, right))

        columns_first()

        @pl.when(is_last)
        def _():
            prepare(w, y, pr, wb, yrow, rrow)

            ends = scaled_blocks((0, 1, REG - 1, REG - 2), sc, wb, yrow, rrow)
            edge[0, 0], edge[0, 1] = with_extras(ends[0], 0), ends[1]
            edge[1, 0], edge[1, 1] = with_extras(ends[2], REG - 1), ends[3]
            pl.semaphore_wait(
                barrier, 1 + has_left.astype(jnp.int32) + has_right.astype(jnp.int32))
            for k, there, where in sides:
                @pl.when(there)
                def _(k=k, where=where):
                    block_copy(k, where).start()

            inner = tuple(range(3, 13))
            blocks = {}
            for r, x in zip(inner, scaled_blocks(inner, sc, wb, yrow, rrow)):
                blocks[r] = block_terms(x, (0, 1, 2))
            for r in EVEN_REGIONS:
                gram[r + 1] = region_gram(r, blocks)
            gram_copy().start()
            for r, x in zip((2, 13), scaled_blocks((2, 13), sc, wb, yrow, rrow)):
                blocks[r] = block_terms(x, (0, 1, 2))
            for r, x in zip((0, 1, 15, 14), ends):
                blocks[r] = block_terms(x, (0, 1, 2))
            for r in (1, 2, 3, 12, 13, 14):
                gram[r + 1] = region_gram(r, blocks)

            for k, there, where in sides:
                @pl.when(there)
                def _(k=k, where=where):
                    block_copy(1 - k, where).wait_recv()
                    block_copy(k, where).wait_send()

                @pl.when(jnp.logical_not(there))
                def _(k=k):
                    halo[k] = jnp.zeros((2, MX, KB), F32)
            blocks[-1] = block_terms(halo[0, 0], (0, 1))
            blocks[-2] = block_terms(halo[0, 1], (0,))
            blocks[16] = block_terms(halo[1, 0], (1, 2))
            blocks[17] = block_terms(halo[1, 1], (2,))
            for r in (-1, 0, 15, 16):
                gram[r + 1] = region_gram(r, blocks)

            items = [item(r) for r in ODD_REGIONS[:8]]
            items += [outside_item(0, 0), outside_item(1, REG + 1)]
            maps = transforms_group(items, gram, ys, zs)
            for k, slab in enumerate(pack(maps[:8]) + [m.astype(BF16) for m in maps[8:]]):
                t[k] = slab
            gram_copy().wait_send()

        @pl.when(jnp.logical_not(is_last))
        def _():
            pl.semaphore_wait(barrier, 1 + (lag < last - 1).astype(jnp.int32))

            @pl.when(lag < last - 1)
            def _():
                pl.semaphore_signal(
                    ready, inc=1, device_id={"lag": lag + 2}, device_id_type=MESH)

        @pl.when(lag == last - 1)
        def _():
            gram_copy().wait_recv()
            maps = transforms_group([item(r) for r in EVEN_REGIONS], gram, ys, zs)
            for k, slab in enumerate(pack(maps)):
                t[7 + k] = slab

        @pl.when(lag >= 2)
        def _():
            pl.semaphore_wait(ready, 1)

        for parity, own, other in ((1, ODD_PIECES, EVEN_PIECES), (0, EVEN_PIECES, ODD_PIECES)):
            @pl.when(odd == parity)
            def _(own=own, other=other):
                for k in range(3):
                    @pl.when(lag < last - 1)
                    def _(k=k):
                        onward(k, own).wait_recv()

                    side(k, own).start()

                    @pl.when(lag >= 2)
                    def _(k=k):
                        onward(k, own).start()

                for k in range(3):
                    side(k, other).wait_recv()
                for k in range(3):
                    side(k, own).wait_send()

                    @pl.when(lag >= 2)
                    def _(k=k):
                        onward(k, own).wait_send()

        t_out[...] = t[...]

    return kernel


def transforms_call(lags, spaces, st, w, y, pr, resample, blend):
    vmem = pl.BlockSpec(memory_space=pltpu.VMEM)
    hbm = pl.BlockSpec(memory_space=pltpu.HBM)
    dma = pltpu.SemaphoreType.DMA
    return pl.pallas_call(
        make_transform_kernel(lags, spaces),
        out_shape=(
            jax.ShapeDtypeStruct((SLABS, M, 128), BF16),
            jax.ShapeDtypeStruct((COLS, 128, 128), BF16),
        ),
        in_specs=[hbm] * 6,
        out_specs=(vmem, vmem),
        scratch_shapes=[
            pltpu.VMEM((LEV, M, COLS), BF16),
            pltpu.VMEM((NOBS, LEV), BF16),
            pltpu.VMEM((NOBS, COLS), F32),
            pltpu.VMEM((NOBS, COLS), F32),
            pltpu.VMEM((REG, M), jnp.int32),
            pltpu.SMEM((REG,), F32),
            pltpu.VMEM((WIDTH * 128, KB), BF16),
            pltpu.VMEM((REG, KB), F32),
            pltpu.VMEM((REG, KB), F32),
            pltpu.VMEM((2, 2, MX, KB), F32),
            pltpu.VMEM((2, 2, MX, KB), F32),
            pltpu.VMEM((REG + 2, MX, 128), F32),
            pltpu.VMEM((SLABS, M, 128), BF16),
            pltpu.VMEM((10, M, 256), BF16),
            pltpu.VMEM((10, M, 256), BF16),
            dma((5,)), dma((4,)), dma((2,)), dma((2,)), dma, dma,
            dma((3,)), dma((3,)), dma((3,)), dma((3,)), pltpu.SemaphoreType.REGULAR,
        ],
        compiler_params=pltpu.CompilerParams(
            collective_id=0, has_side_effects=True, vmem_limit_bytes=24 * 2**20),
    )(*(pltpu.with_memory_space_constraint(x, pltpu.HBM) for x in (st, w, y, pr, resample, blend)))


def analysis_kernel(s, t, near, weight, out, tf, o, ov, o_sem):
    base = lax.axis_index("space") * REG - 1
    slabs = [t[k].astype(F32) for k in range(SLABS)]
    maps = unpack(slabs[:5]) + slabs[5:7] + unpack(slabs[7:])
    for r, m in zip(ODD_REGIONS + EVEN_REGIONS, maps):
        tf[r + 1] = m

    def column(c):
        share = weight[c]
        maps = (share * tf[c // WIDTH + 1] + (1.0 - share) * tf[near[c] - base]).astype(BF16)
        o[c] = jnp.dot(s[c, :, :M], maps, preferred_element_type=F32).astype(BF16)

    for c in range(COLS):
        column(c)

    def store(k):
        first = k * 16
        count = min(16, LEV - first)
        return pltpu.make_async_copy(
            ov.at[pl.ds(first, count)], out.at[pl.ds(first, count)], o_sem.at[k])

    for k in range(8):
        first, stop = k * 16, min(k * 16 + 16, LEV)
        turned = jnp.transpose(o[:, first : first + 16, :M], (1, 2, 0))
        ov[first:stop] = turned[: stop - first]
        store(k).start()
    for k in range(8):
        store(k).wait()


def analysis_call(s, t, near, weight):
    vmem = pl.BlockSpec(memory_space=pltpu.VMEM)
    hbm = pl.BlockSpec(memory_space=pltpu.HBM)
    smem = pl.BlockSpec(memory_space=pltpu.SMEM)
    return pl.pallas_call(
        analysis_kernel,
        out_shape=jax.ShapeDtypeStruct((LEV, M, COLS), BF16),
        in_specs=[vmem, vmem, smem, smem],
        out_specs=hbm,
        scratch_shapes=[
            pltpu.VMEM((REG + 2, M, 128), F32),
            pltpu.VMEM((COLS, 128, 128), BF16),
            pltpu.VMEM((LEV, M, COLS), BF16),
            pltpu.SemaphoreType.DMA((8,)),
        ],
        compiler_params=pltpu.CompilerParams(vmem_limit_bytes=24 * 2**20),
    )(s, t, near, weight)


def per_device(
    states, obs_weights, observations, obs_precision, resample_index, blend_weight,
    stencil_region, stencil_weight,
):
    st = jnp.transpose(states[0], (1, 0, 2))
    t, s = transforms_call(
        lax.axis_size("lag"), lax.axis_size("space"),
        st, obs_weights, observations, obs_precision, resample_index, blend_weight)
    out = analysis_call(s, t, stencil_region, stencil_weight)
    return jnp.transpose(out, (1, 0, 2))[None]


def solution(mesh):
    in_specs = (
        P("lag", None, None, "space"), P(), P(None, "space"), P(None, "space"),
        P("space", None), P("space"), P("space"), P("space"),
    )
    return jax.shard_map(
        per_device, mesh=mesh, in_specs=in_specs, out_specs=P("lag", None, None, "space"),
        check_vma=False)
```

```python
import math

import jax
import jax.numpy as jnp
from jax import lax
from jax.experimental import pallas as pl
from jax.experimental.pallas import tpu as pltpu
from jax.sharding import PartitionSpec as P

M = 80
LEV = 127
NOBS = 24
COLS = 128
WIDTH = 8
REG = 16
NS_ITERS = 8
KB = 256
MX = 96
F32 = jnp.float32
BF16 = jnp.bfloat16
MESH = pl.DeviceIdType.MESH

TAPER = [
    [math.exp(-0.5 * ((q * WIDTH + k - (3 * WIDTH - 1) / 2.0) / WIDTH) ** 2) for k in range(WIDTH)]
    for q in range(3)
]


def split(x):
    high = x.astype(BF16)
    return high, (x - high.astype(F32)).astype(BF16)


def halves(x):
    high, low = split(x)
    return jnp.concatenate([high, low], axis=1)


def product(a, b):
    gap = jnp.zeros((128 - M, 256), BF16)
    out = jnp.dot(a, jnp.concatenate([b, gap, b, gap], axis=0), preferred_element_type=F32)
    return out[:, :128] + out[:, 128:]


def pair_rows(value, spread, chosen):
    first = value.astype(BF16)
    rest = value - first.astype(F32)
    second = rest.astype(BF16)
    third = (rest - second.astype(F32)).astype(BF16)
    dims = (((0,), (0,)), ((), ()))
    total = lax.dot_general(first, spread, dims, preferred_element_type=F32)
    total += lax.dot_general(second, spread, dims, preferred_element_type=F32)
    total += lax.dot_general(third, spread, dims, preferred_element_type=F32)
    return jnp.sum(jnp.where(chosen, total, 0.0).reshape(REG, WIDTH, KB), axis=1)


def prepare(w, y, pr, wb, yrow, rrow):
    row = lax.broadcasted_iota(jnp.int32, (NOBS, KB), 0)
    lane = lax.broadcasted_iota(jnp.int32, (NOBS, KB), 1)
    spread = jnp.where((lane % NOBS == row) & (lane < WIDTH * NOBS), 1.0, 0.0).astype(BF16)
    row = lax.broadcasted_iota(jnp.int32, (COLS, KB), 0)
    lane = lax.broadcasted_iota(jnp.int32, (COLS, KB), 1)
    chosen = lane // NOBS == row % WIDTH
    yrow[...] = pair_rows(y[...], spread, chosen)
    rrow[...] = pair_rows(jnp.sqrt(pr[...]), spread, chosen)
    wide = lax.dot_general(w[...], spread, (((0,), (0,)), ((), ())), preferred_element_type=F32)
    wide = jnp.concatenate([wide, jnp.zeros((1, KB), F32)], axis=0)
    for k in range(WIDTH):
        wb[k * 128 : (k + 1) * 128] = jnp.where(lane // NOBS == k, wide, 0.0).astype(BF16)


def scaled_blocks(regions, sc, wb, yrow, rrow):
    rows = []
    for r in regions:
        turned = jnp.transpose(sc[pl.ds(r * WIDTH, WIDTH)], (0, 2, 1))[:, :M]
        rows.append(jnp.concatenate([turned[k] for k in range(WIDTH)], axis=1))
    out = jnp.dot(jnp.concatenate(rows, axis=0), wb[...], preferred_element_type=F32)
    top = lax.broadcasted_iota(jnp.int32, (MX - M, KB), 0) == 0
    blocks = []
    for k, r in enumerate(regions):
        obs = out[k * M : (k + 1) * M]
        mean = jnp.sum(obs, axis=0, keepdims=True) * (1.0 / M)
        innovation = jnp.where(top, yrow[pl.ds(r, 1), :] - mean, 0.0)
        blocks.append(
            jnp.concatenate([obs - mean, innovation], axis=0) * rrow[pl.ds(r, 1), :]
        )
    return blocks


def block_terms(x, parts):
    left = split(x)
    across = jnp.concatenate([x, jnp.zeros((128 - MX, KB), F32)], axis=0).T
    gap = jnp.zeros((KB - WIDTH * NOBS, 128), F32)
    terms = {}
    for q in parts:
        tapered = [across[k * NOBS : (k + 1) * NOBS] * TAPER[q][k] for k in range(WIDTH)]
        terms[q] = (*left, halves(jnp.concatenate(tapered + [gap], axis=0)))
    return terms


def gram_of(terms):
    high, low, right = zip(*terms)
    right = jnp.concatenate(right, axis=0)
    out = jnp.dot(jnp.concatenate(high, axis=1), right, preferred_element_type=F32)
    out2 = jnp.dot(jnp.concatenate(low, axis=1), right[:, :128], preferred_element_type=F32)
    return out[:, :128] + out[:, 128:] + out2


def region_gram(r, blocks):
    return gram_of([blocks[r - 1 + q][q] for q in range(3)])


def transforms_group(items, gram, ys, zs):
    row = lax.broadcasted_iota(jnp.int32, (M, 128), 0)
    col = lax.broadcasted_iota(jnp.int32, (M, 128), 1)
    eye = (row == col).astype(F32)
    count = len(items)
    norms = []
    for k, (slot, _, _) in enumerate(items):
        cross = jnp.where(col < M, gram[slot, :M, :], 0.0)
        square = jnp.sum(cross * cross, axis=0, keepdims=True)
        norm = 1.0 + jnp.sqrt(jnp.sum(square, axis=1, keepdims=True)) * (1.0 / (M - 1))
        norms.append(norm)
        y = (eye + cross * (1.0 / (M - 1))) / norm
        e = halves(1.5 * eye - 0.5 * y)
        ys[k] = halves(product(halves(y), e))
        zs[k] = e

    @pl.loop(0, NS_ITERS - 2)
    def _(sweep):
        factors = [halves(1.5 * eye - 0.5 * product(zs[k], ys[k])) for k in range(count)]
        for k in range(count):
            both = product(jnp.concatenate([ys[k], zs[k]], axis=0), factors[k])
            ys[k] = halves(both[:M])
            zs[k] = halves(both[M:])

    result = []
    for k, (slot, drawn_row, share) in enumerate(items):
        e = halves(1.5 * eye - 0.5 * product(zs[k], ys[k]))
        root = product(zs[k], e) / jnp.sqrt(norms[k])
        drive = gram[slot, :M, M : M + 1]
        half = jnp.sum(root * drive, axis=0, keepdims=True)
        mean_weight = jnp.sum(root * half, axis=1, keepdims=True) * (1.0 / (M - 1))
        weights = mean_weight + root
        etkf = 1.0 / M + weights - jnp.sum(weights, axis=0, keepdims=True) * (1.0 / M)
        drawn = (drawn_row == row).astype(F32)
        result.append((1.0 - share) * etkf + share * drawn)
    return result


def pack(maps):
    lane = lax.broadcasted_iota(jnp.int32, (M, 128), 1)
    a, b, c, d, e, f, g, h = maps

    def tail(first, second=None, cut=128):
        return first if second is None else jnp.where(lane < cut, first, second)

    spare = (
        pltpu.roll(f, 80, 1),
        tail(pltpu.roll(f, 32, 1), pltpu.roll(g, 112, 1), 112),
        pltpu.roll(g, 64, 1),
        tail(pltpu.roll(g, 16, 1), pltpu.roll(h, 96, 1), 96),
        pltpu.roll(h, 48, 1),
    )
    return [
        jnp.where(lane < M, kept, extra).astype(BF16)
        for kept, extra in zip((a, b, c, d, e), spare)
    ]


def unpack(slabs):
    lane = lax.broadcasted_iota(jnp.int32, (M, 128), 1)
    a, b, c, d, e = slabs
    f = jnp.where(lane < 48, pltpu.roll(a, 48, 1), pltpu.roll(b, 96, 1))
    g = jnp.where(
        lane < 16, pltpu.roll(b, 16, 1),
        jnp.where(lane < 64, pltpu.roll(c, 64, 1), pltpu.roll(d, 112, 1)))
    h = jnp.where(lane < 32, pltpu.roll(d, 32, 1), pltpu.roll(e, 80, 1))
    return [a, b, c, d, e, f, g, h]


ODD_REGIONS = (12, 13, 14, 15, 16, 1, 2, 3)
LATE_REGIONS = (-1, 0)
EVEN_REGIONS = (4, 5, 6, 7, 8, 9, 10, 11)
SLABS = 12
PIECES = ((0, 3), (3, 2))
LEVEL_CHUNKS = ((0, 32), (32, 32), (64, 32), (96, 31))


def make_transform_kernel(lags, spaces):
    last = lags - 1

    def kernel(
        st_hbm, w_hbm, y_hbm, pr_hbm, resample_hbm, blend_hbm, t_out, sc,
        st, w, y, pr, resample, blend,
        wb, yrow, rrow, edge, halo, gram, t, ys, zs,
        in_sem, st_sem, x_send, x_recv, g_send, g_recv,
        p_next, p_side, own_recv, other_recv, f_send, f_recv, ready,
    ):
        lag = lax.axis_index("lag")
        here = lax.axis_index("space")
        odd = lax.rem(lag, 2)
        sibling = lag + 1 - 2 * odd
        has_left, has_right = here > 0, here < spaces - 1
        left, right = here - 1, here + 1
        barrier = pltpu.get_barrier_semaphore()
        is_last = lag == last

        def greet(where):
            pl.semaphore_signal(barrier, inc=1, device_id=where, device_id_type=MESH)

        greet({"lag": sibling})

        @pl.when(lag >= last - 1)
        def _():
            for back in (6, 4, 2):
                greet({"lag": lag - back})

        @pl.when(is_last)
        def _():
            @pl.when(has_left)
            def _():
                greet({"space": left})

            @pl.when(has_right)
            def _():
                greet({"space": right})

        def level_copy(k):
            first, count = LEVEL_CHUNKS[k]
            return pltpu.make_async_copy(
                st_hbm.at[pl.ds(first, count)], st.at[pl.ds(first, count)], st_sem.at[k])

        small = [
            pltpu.make_async_copy(src, dst, in_sem.at[k])
            for k, (src, dst) in enumerate(
                ((w_hbm, w), (y_hbm, y), (pr_hbm, pr), (resample_hbm, resample), (blend_hbm, blend)))
        ]
        for copy in small:
            copy.start()
        for k in range(len(LEVEL_CHUNKS)):
            level_copy(k).start()
        for copy in small:
            copy.wait()

        def columns_first():
            gap = jnp.zeros((1, M, COLS), BF16)
            for k, (first, count) in enumerate(LEVEL_CHUNKS):
                level_copy(k).wait()
                for j in range(first, first + count, 16):
                    part = st[j : min(j + 16, LEV)]
                    if j + 16 > LEV:
                        part = jnp.concatenate([part, gap], axis=0)
                    sc[:, j : j + 16, :M] = jnp.transpose(part, (2, 0, 1))

        def side(k, first):
            ref = t.at[pl.ds(first + PIECES[k][0], PIECES[k][1])]
            return pltpu.make_async_remote_copy(
                src_ref=ref, dst_ref=ref, send_sem=p_side.at[k], recv_sem=other_recv.at[k],
                device_id={"lag": sibling}, device_id_type=MESH)

        def direct(k, first, back):
            ref = t.at[pl.ds(first + PIECES[k][0], PIECES[k][1])]
            return pltpu.make_async_remote_copy(
                src_ref=ref, dst_ref=ref, send_sem=p_next.at[k, back // 2 - 1],
                recv_sem=own_recv.at[k], device_id={"lag": lag - back}, device_id_type=MESH)

        def late(back):
            ref = t.at[pl.ds(5, 2)]
            return pltpu.make_async_remote_copy(
                src_ref=ref, dst_ref=ref, send_sem=f_send.at[back // 2], recv_sem=f_recv,
                device_id={"lag": lag - back}, device_id_type=MESH)

        def each_direct(first, act):
            for back in (6, 4, 2):
                for k in range(len(PIECES)):
                    act(direct(k, first, back))

        def each_side(first, act):
            for k in range(len(PIECES)):
                act(side(k, first))

        def start(copy):
            copy.start()

        def sent(copy):
            copy.wait_send()

        def arrived(copy):
            copy.wait_recv()

        def block_copy(k, where):
            return pltpu.make_async_remote_copy(
                src_ref=edge.at[k], dst_ref=halo.at[1 - k], send_sem=x_send.at[k],
                recv_sem=x_recv.at[1 - k], device_id={"space": where}, device_id_type=MESH)

        def gram_copy():
            ref = gram.at[pl.ds(5, 8)]
            return pltpu.make_async_remote_copy(
                src_ref=ref, dst_ref=ref, send_sem=g_send, recv_sem=g_recv,
                device_id={"lag": sibling}, device_id_type=MESH)

        def drawn_row(r):
            return resample[r : r + 1, :]

        def wide_row(r):
            return jnp.concatenate([drawn_row(r), jnp.full((1, 48), -1, jnp.int32)], axis=1)

        def item(r):
            return (r + 1, wide_row(r), blend[r])

        def payload(near, far, r):
            values = jnp.concatenate(
                [drawn_row(r).astype(F32), jnp.zeros((1, KB - M), F32)], axis=1)
            which = lax.broadcasted_iota(jnp.int32, (88, KB), 0)
            near = jnp.where(
                which == M + 1, values, jnp.where(which == M + 2, blend[r], near[:88]))
            lane = lax.broadcasted_iota(jnp.int32, (88, 128), 1)
            both = jnp.where(lane < 64, near[:, 128:], pltpu.roll(far[:88, 128:], 64, 1))
            return jnp.concatenate([near[:, :128], both, far[:88, :128]], axis=1)

        def received(k):
            lane = lax.broadcasted_iota(jnp.int32, (88, 128), 1)
            both = halo[k, :, 128:256]
            near = jnp.concatenate([halo[k, :, :128], jnp.where(lane < 64, both, 0.0)], axis=1)
            far = jnp.concatenate(
                [halo[k, :, 256:], jnp.where(lane < 64, pltpu.roll(both, 64, 1), 0.0)], axis=1)
            gap = jnp.zeros((MX - 88, KB), F32)
            return (jnp.concatenate([near, gap], axis=0), jnp.concatenate([far, gap], axis=0))

        def await_halo(k):
            there, where = ((has_left, left), (has_right, right))[k]

            @pl.when(there)
            def _():
                block_copy(1 - k, where).wait_recv()
                block_copy(k, where).wait_send()

            @pl.when(jnp.logical_not(there))
            def _():
                halo[k] = jnp.zeros((88, 384), F32)

        def outside_item(k, slot):
            drawn = halo[k, M + 1 : M + 2, :128].astype(jnp.int32)
            return (slot, drawn, halo[k, M + 2 : M + 3, :128])

        sides = ((0, has_left, left), (1, has_right, right))

        @pl.when(is_last)
        def _():
            prepare(w, y, pr, wb, yrow, rrow)

        columns_first()

        @pl.when(is_last)
        def _():

            ends = scaled_blocks((0, 1, REG - 1, REG - 2), sc, wb, yrow, rrow)
            edge[0] = payload(ends[0], ends[1], 0)
            edge[1] = payload(ends[2], ends[3], REG - 1)
            pl.semaphore_wait(
                barrier, 1 + has_left.astype(jnp.int32) + has_right.astype(jnp.int32))
            for k, there, where in sides:
                @pl.when(there)
                def _(k=k, where=where):
                    block_copy(k, where).start()

            inner = tuple(range(3, 13))
            blocks = {}
            for r, x in zip(inner, scaled_blocks(inner, sc, wb, yrow, rrow)):
                blocks[r] = block_terms(x, (0, 1, 2))
            for r in EVEN_REGIONS:
                gram[r + 1] = region_gram(r, blocks)
            gram_copy().start()
            for r, x in zip((2, 13), scaled_blocks((2, 13), sc, wb, yrow, rrow)):
                blocks[r] = block_terms(x, (0, 1, 2))
            for r, x in zip((0, 1, 15, 14), ends):
                blocks[r] = block_terms(x, (0, 1, 2))
            for r in (1, 2, 3, 12, 13, 14):
                gram[r + 1] = region_gram(r, blocks)

            await_halo(1)
            near, far = received(1)
            blocks[16] = block_terms(near, (1, 2))
            blocks[17] = block_terms(far, (2,))
            for r in (15, 16):
                gram[r + 1] = region_gram(r, blocks)

            items = [outside_item(1, 17) if r == 16 else item(r) for r in ODD_REGIONS]
            for k, slab in enumerate(pack(transforms_group(items, gram, ys, zs))):
                t[k] = slab
            gram_copy().wait_send()
            pl.semaphore_wait(ready, 3)
            each_side(0, start)
            each_direct(0, start)

            await_halo(0)
            near, far = received(0)
            blocks[-1] = block_terms(near, (0, 1))
            blocks[-2] = block_terms(far, (0,))
            for r in LATE_REGIONS:
                gram[r + 1] = region_gram(r, blocks)
            items = [outside_item(0, 0), item(0)]
            for k, m in enumerate(transforms_group(items, gram, ys, zs)):
                t[5 + k] = m.astype(BF16)
            for back in (6, 4, 2, 1):
                late(back).start()
            each_side(7, arrived)
            each_direct(0, sent)
            each_side(0, sent)
            for back in (6, 4, 2, 1):
                late(back).wait_send()

        @pl.when(lag == last - 1)
        def _():
            pl.semaphore_wait(barrier, 1)
            gram_copy().wait_recv()
            maps = transforms_group([item(r) for r in EVEN_REGIONS], gram, ys, zs)
            for k, slab in enumerate(pack(maps)):
                t[7 + k] = slab
            pl.semaphore_wait(ready, 3)
            each_side(7, start)
            each_direct(7, start)
            each_side(0, arrived)
            late(1).wait_recv()
            each_direct(7, sent)
            each_side(7, sent)

        @pl.when(lag < last - 1)
        def _():
            pl.semaphore_wait(barrier, 2)
            pl.semaphore_signal(
                ready, inc=1, device_id={"lag": last - 1 + odd}, device_id_type=MESH)
            for parity, own, other in ((1, 0, 7), (0, 7, 0)):
                @pl.when(odd == parity)
                def _(parity=parity, own=own, other=other):
                    for k in range(len(PIECES)):
                        direct(k, own, 2).wait_recv()
                        side(k, own).start()
                    each_side(other, arrived)
                    late(1).wait_recv()
                    if parity == 1:
                        late(1).start()
                    each_side(own, sent)
                    if parity == 1:
                        late(1).wait_send()

        t_out[...] = t[...]

    return kernel


def transforms_call(lags, spaces, st, w, y, pr, resample, blend):
    vmem = pl.BlockSpec(memory_space=pltpu.VMEM)
    hbm = pl.BlockSpec(memory_space=pltpu.HBM)
    dma = pltpu.SemaphoreType.DMA
    return pl.pallas_call(
        make_transform_kernel(lags, spaces),
        out_shape=(
            jax.ShapeDtypeStruct((SLABS, M, 128), BF16),
            jax.ShapeDtypeStruct((COLS, 128, 128), BF16),
        ),
        in_specs=[hbm] * 6,
        out_specs=(vmem, vmem),
        scratch_shapes=[
            pltpu.VMEM((LEV, M, COLS), BF16),
            pltpu.VMEM((NOBS, LEV), BF16),
            pltpu.VMEM((NOBS, COLS), F32),
            pltpu.VMEM((NOBS, COLS), F32),
            pltpu.VMEM((REG, M), jnp.int32),
            pltpu.SMEM((REG,), F32),
            pltpu.VMEM((WIDTH * 128, KB), BF16),
            pltpu.VMEM((REG, KB), F32),
            pltpu.VMEM((REG, KB), F32),
            pltpu.VMEM((2, 88, 384), F32),
            pltpu.VMEM((2, 88, 384), F32),
            pltpu.VMEM((REG + 2, MX, 128), F32),
            pltpu.VMEM((SLABS, M, 128), BF16),
            pltpu.VMEM((8, M, 256), BF16),
            pltpu.VMEM((8, M, 256), BF16),
            dma((5,)), dma((4,)), dma((2,)), dma((2,)), dma, dma,
            dma((2, 3)), dma((2,)), dma((2,)), dma((2,)), dma((4,)), dma,
            pltpu.SemaphoreType.REGULAR,
        ],
        compiler_params=pltpu.CompilerParams(
            collective_id=0, has_side_effects=True, vmem_limit_bytes=24 * 2**20),
    )(*(pltpu.with_memory_space_constraint(x, pltpu.HBM) for x in (st, w, y, pr, resample, blend)))


def analysis_kernel(s, t, near, weight, out, tf, o, ov, o_sem):
    base = lax.axis_index("space") * REG - 1
    slabs = [t[k].astype(F32) for k in range(SLABS)]
    maps = unpack(slabs[:5]) + slabs[5:7] + unpack(slabs[7:])
    for r, m in zip(ODD_REGIONS + LATE_REGIONS + EVEN_REGIONS, maps):
        tf[r + 1] = m

    def column(c):
        share = weight[c]
        maps = (share * tf[c // WIDTH + 1] + (1.0 - share) * tf[near[c] - base]).astype(BF16)
        o[c] = jnp.dot(s[c, :, :M], maps, preferred_element_type=F32).astype(BF16)

    for c in range(COLS):
        column(c)

    def store(k):
        first = k * 16
        count = min(16, LEV - first)
        return pltpu.make_async_copy(
            ov.at[pl.ds(first, count)], out.at[pl.ds(first, count)], o_sem.at[k])

    for k in range(8):
        first, stop = k * 16, min(k * 16 + 16, LEV)
        turned = jnp.transpose(o[:, first : first + 16, :M], (1, 2, 0))
        ov[first:stop] = turned[: stop - first]
        store(k).start()
    for k in range(8):
        store(k).wait()


def analysis_call(s, t, near, weight):
    vmem = pl.BlockSpec(memory_space=pltpu.VMEM)
    hbm = pl.BlockSpec(memory_space=pltpu.HBM)
    smem = pl.BlockSpec(memory_space=pltpu.SMEM)
    return pl.pallas_call(
        analysis_kernel,
        out_shape=jax.ShapeDtypeStruct((LEV, M, COLS), BF16),
        in_specs=[vmem, vmem, smem, smem],
        out_specs=hbm,
        scratch_shapes=[
            pltpu.VMEM((REG + 2, M, 128), F32),
            pltpu.VMEM((COLS, 128, 128), BF16),
            pltpu.VMEM((LEV, M, COLS), BF16),
            pltpu.SemaphoreType.DMA((8,)),
        ],
        compiler_params=pltpu.CompilerParams(vmem_limit_bytes=24 * 2**20),
    )(s, t, near, weight)


def per_device(
    states, obs_weights, observations, obs_precision, resample_index, blend_weight,
    stencil_region, stencil_weight,
):
    st = jnp.transpose(states[0], (1, 0, 2))
    t, s = transforms_call(
        lax.axis_size("lag"), lax.axis_size("space"),
        st, obs_weights, observations, obs_precision, resample_index, blend_weight)
    out = analysis_call(s, t, stencil_region, stencil_weight)
    return jnp.transpose(out, (1, 0, 2))[None]


def solution(mesh):
    in_specs = (
        P("lag", None, None, "space"), P(), P(None, "space"), P(None, "space"),
        P("space", None), P("space"), P("space"), P("space"),
    )
    return jax.shard_map(
        per_device, mesh=mesh, in_specs=in_specs, out_specs=P("lag", None, None, "space"),
        check_vma=False)
```

```python
import math

import jax
import jax.numpy as jnp
from jax import lax
from jax.experimental import pallas as pl
from jax.experimental.pallas import tpu as pltpu
from jax.sharding import PartitionSpec as P

M = 80
LEV = 127
NOBS = 24
COLS = 128
WIDTH = 8
REG = 16
NS_ITERS = 8
KB = 256
MX = 96
F32 = jnp.float32
BF16 = jnp.bfloat16
MESH = pl.DeviceIdType.MESH

TAPER = [
    [math.exp(-0.5 * ((q * WIDTH + k - (3 * WIDTH - 1) / 2.0) / WIDTH) ** 2) for k in range(WIDTH)]
    for q in range(3)
]


def split(x):
    high = x.astype(BF16)
    return high, (x - high.astype(F32)).astype(BF16)


def halves(x):
    high, low = split(x)
    return jnp.concatenate([high, low], axis=1)


def product(a, b):
    gap = jnp.zeros((128 - M, 256), BF16)
    out = jnp.dot(a, jnp.concatenate([b, gap, b, gap], axis=0), preferred_element_type=F32)
    return out[:, :128] + out[:, 128:]


def pair_rows(value, spread, chosen):
    first = value.astype(BF16)
    rest = value - first.astype(F32)
    second = rest.astype(BF16)
    third = (rest - second.astype(F32)).astype(BF16)
    dims = (((0,), (0,)), ((), ()))
    total = lax.dot_general(first, spread, dims, preferred_element_type=F32)
    total += lax.dot_general(second, spread, dims, preferred_element_type=F32)
    total += lax.dot_general(third, spread, dims, preferred_element_type=F32)
    return jnp.sum(jnp.where(chosen, total, 0.0).reshape(REG, WIDTH, KB), axis=1)


def prepare(w, y, pr, wb, yrow, rrow):
    row = lax.broadcasted_iota(jnp.int32, (NOBS, KB), 0)
    lane = lax.broadcasted_iota(jnp.int32, (NOBS, KB), 1)
    spread = jnp.where((lane % NOBS == row) & (lane < WIDTH * NOBS), 1.0, 0.0).astype(BF16)
    row = lax.broadcasted_iota(jnp.int32, (COLS, KB), 0)
    lane = lax.broadcasted_iota(jnp.int32, (COLS, KB), 1)
    chosen = lane // NOBS == row % WIDTH
    yrow[...] = pair_rows(y[...], spread, chosen)
    rrow[...] = pair_rows(jnp.sqrt(pr[...]), spread, chosen)
    wide = lax.dot_general(w[...], spread, (((0,), (0,)), ((), ())), preferred_element_type=F32)
    wide = jnp.concatenate([wide, jnp.zeros((1, KB), F32)], axis=0)
    for k in range(WIDTH):
        wb[k * 128 : (k + 1) * 128] = jnp.where(lane // NOBS == k, wide, 0.0).astype(BF16)


def scaled_blocks(regions, sc, wb, yrow, rrow):
    rows = []
    for r in regions:
        turned = jnp.transpose(sc[pl.ds(r * WIDTH, WIDTH)], (0, 2, 1))[:, :M]
        rows.append(jnp.concatenate([turned[k] for k in range(WIDTH)], axis=1))
    out = jnp.dot(jnp.concatenate(rows, axis=0), wb[...], preferred_element_type=F32)
    top = lax.broadcasted_iota(jnp.int32, (MX - M, KB), 0) == 0
    blocks = []
    for k, r in enumerate(regions):
        obs = out[k * M : (k + 1) * M]
        mean = jnp.sum(obs, axis=0, keepdims=True) * (1.0 / M)
        innovation = jnp.where(top, yrow[pl.ds(r, 1), :] - mean, 0.0)
        blocks.append(
            jnp.concatenate([obs - mean, innovation], axis=0) * rrow[pl.ds(r, 1), :]
        )
    return blocks


def block_terms(x, parts):
    left = split(x)
    across = jnp.concatenate([x, jnp.zeros((128 - MX, KB), F32)], axis=0).T
    gap = jnp.zeros((KB - WIDTH * NOBS, 128), F32)
    terms = {}
    for q in parts:
        tapered = [across[k * NOBS : (k + 1) * NOBS] * TAPER[q][k] for k in range(WIDTH)]
        terms[q] = (*left, halves(jnp.concatenate(tapered + [gap], axis=0)))
    return terms


def gram_of(terms):
    high, low, right = zip(*terms)
    right = jnp.concatenate(right, axis=0)
    out = jnp.dot(jnp.concatenate(high, axis=1), right, preferred_element_type=F32)
    out2 = jnp.dot(jnp.concatenate(low, axis=1), right[:, :128], preferred_element_type=F32)
    return out[:, :128] + out[:, 128:] + out2


def region_gram(r, blocks):
    return gram_of([blocks[r - 1 + q][q] for q in range(3)])


def transforms_group(items, gram, ys, zs):
    row = lax.broadcasted_iota(jnp.int32, (M, 128), 0)
    col = lax.broadcasted_iota(jnp.int32, (M, 128), 1)
    eye = (row == col).astype(F32)
    count = len(items)
    norms = []
    for k, (slot, _, _) in enumerate(items):
        cross = jnp.where(col < M, gram[slot, :M, :], 0.0)
        square = jnp.sum(cross * cross, axis=0, keepdims=True)
        norm = 1.0 + jnp.sqrt(jnp.sum(square, axis=1, keepdims=True)) * (1.0 / (M - 1))
        norms.append(norm)
        y = (eye + cross * (1.0 / (M - 1))) / norm
        e = halves(1.5 * eye - 0.5 * y)
        ys[k] = halves(product(halves(y), e))
        zs[k] = e

    @pl.loop(0, NS_ITERS - 2)
    def _(sweep):
        factors = [halves(1.5 * eye - 0.5 * product(zs[k], ys[k])) for k in range(count)]
        for k in range(count):
            both = product(jnp.concatenate([ys[k], zs[k]], axis=0), factors[k])
            ys[k] = halves(both[:M])
            zs[k] = halves(both[M:])

    result = []
    for k, (slot, drawn_row, share) in enumerate(items):
        e = halves(1.5 * eye - 0.5 * product(zs[k], ys[k]))
        root = product(zs[k], e) / jnp.sqrt(norms[k])
        drive = gram[slot, :M, M : M + 1]
        half = jnp.sum(root * drive, axis=0, keepdims=True)
        mean_weight = jnp.sum(root * half, axis=1, keepdims=True) * (1.0 / (M - 1))
        weights = mean_weight + root
        etkf = 1.0 / M + weights - jnp.sum(weights, axis=0, keepdims=True) * (1.0 / M)
        drawn = (drawn_row == row).astype(F32)
        result.append((1.0 - share) * etkf + share * drawn)
    return result


def pack(maps):
    lane = lax.broadcasted_iota(jnp.int32, (M, 128), 1)
    a, b, c, d, e, f, g, h = maps

    def tail(first, second=None, cut=128):
        return first if second is None else jnp.where(lane < cut, first, second)

    spare = (
        pltpu.roll(f, 80, 1),
        tail(pltpu.roll(f, 32, 1), pltpu.roll(g, 112, 1), 112),
        pltpu.roll(g, 64, 1),
        tail(pltpu.roll(g, 16, 1), pltpu.roll(h, 96, 1), 96),
        pltpu.roll(h, 48, 1),
    )
    return [
        jnp.where(lane < M, kept, extra).astype(BF16)
        for kept, extra in zip((a, b, c, d, e), spare)
    ]


def unpack(slabs):
    lane = lax.broadcasted_iota(jnp.int32, (M, 128), 1)
    a, b, c, d, e = slabs
    f = jnp.where(lane < 48, pltpu.roll(a, 48, 1), pltpu.roll(b, 96, 1))
    g = jnp.where(
        lane < 16, pltpu.roll(b, 16, 1),
        jnp.where(lane < 64, pltpu.roll(c, 64, 1), pltpu.roll(d, 112, 1)))
    h = jnp.where(lane < 32, pltpu.roll(d, 32, 1), pltpu.roll(e, 80, 1))
    return [a, b, c, d, e, f, g, h]


ODD_REGIONS = (12, 13, 14, 15, 16, 1, 2, 3)
LATE_REGIONS = (-1, 0)
EVEN_REGIONS = (4, 5, 6, 7, 8, 9, 10, 11)
SLABS = 12
PIECES = ((0, 3), (3, 2))
LEVEL_CHUNKS = ((0, 32), (32, 32), (64, 32), (96, 31))


def analyse(c, base, near, weight, maps, states, out):
    share = weight[c]
    mixed = share * maps[c // WIDTH + 1] + (1.0 - share) * maps[jnp.clip(near[c] - base, 0, maps.shape[0] - 1)]
    out[c] = jnp.dot(states[c, :, :M], mixed.astype(BF16), preferred_element_type=F32).astype(BF16)


def make_transform_kernel(lags, spaces):
    last = lags - 1

    def kernel(
        st_hbm, w_hbm, y_hbm, pr_hbm, resample_hbm, blend_hbm, near_hbm, weight_hbm, t_out, sc,
        st, w, y, pr, resample, blend, near, weight, tf,
        wb, yrow, rrow, edge, halo, gram, t, ys, zs,
        in_sem, st_sem, x_send, x_recv, g_send, g_recv,
        p_next, p_side, own_recv, other_recv, f_send, f_recv, ready,
    ):
        lag = lax.axis_index("lag")
        here = lax.axis_index("space")
        odd = lax.rem(lag, 2)
        sibling = lag + 1 - 2 * odd
        has_left, has_right = here > 0, here < spaces - 1
        left, right = here - 1, here + 1
        barrier = pltpu.get_barrier_semaphore()
        is_last = lag == last

        def greet(where):
            pl.semaphore_signal(barrier, inc=1, device_id=where, device_id_type=MESH)

        greet({"lag": sibling})

        @pl.when(lag >= last - 1)
        def _():
            for back in (6, 4, 2):
                greet({"lag": lag - back})

        @pl.when((lag == 2) | (lag == 3))
        def _():
            greet({"lag": lag + 2})

        @pl.when(is_last)
        def _():
            @pl.when(has_left)
            def _():
                greet({"space": left})

            @pl.when(has_right)
            def _():
                greet({"space": right})

        def level_copy(k):
            first, count = LEVEL_CHUNKS[k]
            return pltpu.make_async_copy(
                st_hbm.at[pl.ds(first, count)], st.at[pl.ds(first, count)], st_sem.at[k])

        small = [
            pltpu.make_async_copy(src, dst, in_sem.at[k])
            for k, (src, dst) in enumerate(
                ((w_hbm, w), (y_hbm, y), (pr_hbm, pr), (resample_hbm, resample), (blend_hbm, blend),
                 (near_hbm, near), (weight_hbm, weight)))
        ]
        for copy in small:
            copy.start()
        for k in range(len(LEVEL_CHUNKS)):
            level_copy(k).start()
        for copy in small:
            copy.wait()

        def columns_first():
            gap = jnp.zeros((1, M, COLS), BF16)
            for k, (first, count) in enumerate(LEVEL_CHUNKS):
                level_copy(k).wait()
                for j in range(first, first + count, 16):
                    part = st[j : min(j + 16, LEV)]
                    if j + 16 > LEV:
                        part = jnp.concatenate([part, gap], axis=0)
                    sc[:, j : j + 16, :M] = jnp.transpose(part, (2, 0, 1))

        def side(k, first):
            ref = t.at[pl.ds(first + PIECES[k][0], PIECES[k][1])]
            return pltpu.make_async_remote_copy(
                src_ref=ref, dst_ref=ref, send_sem=p_side.at[k], recv_sem=other_recv.at[k],
                device_id={"lag": sibling}, device_id_type=MESH)

        def direct(k, first, back):
            ref = t.at[pl.ds(first + PIECES[k][0], PIECES[k][1])]
            return pltpu.make_async_remote_copy(
                src_ref=ref, dst_ref=ref, send_sem=p_next.at[k, back // 2 - 1],
                recv_sem=own_recv.at[k], device_id={"lag": lag - back}, device_id_type=MESH)

        def late(back):
            ref = t.at[pl.ds(5, 2)]
            return pltpu.make_async_remote_copy(
                src_ref=ref, dst_ref=ref, send_sem=f_send.at[back // 2], recv_sem=f_recv,
                device_id={"lag": lag - back}, device_id_type=MESH)

        def each_direct(first, act):
            for back in (2, 6):
                for k in range(len(PIECES)):
                    act(direct(k, first, back))

        def each_side(first, act):
            for k in range(len(PIECES)):
                act(side(k, first))

        def start(copy):
            copy.start()

        def sent(copy):
            copy.wait_send()

        def arrived(copy):
            copy.wait_recv()

        def block_copy(k, where):
            return pltpu.make_async_remote_copy(
                src_ref=edge.at[k], dst_ref=halo.at[1 - k], send_sem=x_send.at[k],
                recv_sem=x_recv.at[1 - k], device_id={"space": where}, device_id_type=MESH)

        def gram_copy():
            ref = gram.at[pl.ds(5, 8)]
            return pltpu.make_async_remote_copy(
                src_ref=ref, dst_ref=ref, send_sem=g_send, recv_sem=g_recv,
                device_id={"lag": sibling}, device_id_type=MESH)

        def drawn_row(r):
            return resample[r : r + 1, :]

        def wide_row(r):
            return jnp.concatenate([drawn_row(r), jnp.full((1, 48), -1, jnp.int32)], axis=1)

        def item(r):
            return (r + 1, wide_row(r), blend[r])

        def with_extras(partial, r):
            values = jnp.concatenate(
                [drawn_row(r).astype(F32), jnp.zeros((1, 128 - M), F32)], axis=1)
            which = lax.broadcasted_iota(jnp.int32, (MX, 128), 0)
            return jnp.where(
                which == M + 1, values, jnp.where(which == M + 2, blend[r], partial))

        def await_halo(k):
            there, where = ((has_left, left), (has_right, right))[k]

            @pl.when(there)
            def _():
                block_copy(1 - k, where).wait_recv()
                block_copy(k, where).wait_send()

            @pl.when(jnp.logical_not(there))
            def _():
                halo[k] = jnp.zeros((2, MX, 128), F32)

        def outside_item(k, slot):
            drawn = halo[k, 1, M + 1 : M + 2, :].astype(jnp.int32)
            return (slot, drawn, halo[k, 1, M + 2 : M + 3, :])

        sides = ((0, has_left, left), (1, has_right, right))

        @pl.when(is_last)
        def _():
            prepare(w, y, pr, wb, yrow, rrow)

        columns_first()

        @pl.when(is_last)
        def _():

            ends = scaled_blocks((0, 1, REG - 1, REG - 2), sc, wb, yrow, rrow)
            blocks = {}
            for r, x in zip((0, 1, 15, 14), ends):
                blocks[r] = block_terms(x, (0, 1, 2))
            edge[0, 0] = gram_of([blocks[0][2]])
            edge[0, 1] = with_extras(gram_of([blocks[0][1], blocks[1][2]]), 0)
            edge[1, 0] = gram_of([blocks[15][0]])
            edge[1, 1] = with_extras(gram_of([blocks[14][0], blocks[15][1]]), REG - 1)
            pl.semaphore_wait(
                barrier, 1 + has_left.astype(jnp.int32) + has_right.astype(jnp.int32))
            for k, there, where in sides:
                @pl.when(there)
                def _(k=k, where=where):
                    block_copy(k, where).start()

            inner = tuple(range(3, 13))
            for r, x in zip(inner, scaled_blocks(inner, sc, wb, yrow, rrow)):
                blocks[r] = block_terms(x, (0, 1, 2))
            for r in EVEN_REGIONS:
                gram[r + 1] = region_gram(r, blocks)
            gram_copy().start()
            for r, x in zip((2, 13), scaled_blocks((2, 13), sc, wb, yrow, rrow)):
                blocks[r] = block_terms(x, (0, 1, 2))
            for r in (1, 2, 3, 12, 13, 14):
                gram[r + 1] = region_gram(r, blocks)

            await_halo(1)
            gram[REG] = edge[1, 1] + halo[1, 0]
            gram[REG + 1] = edge[1, 0] + halo[1, 1]

            items = [outside_item(1, 17) if r == 16 else item(r) for r in ODD_REGIONS]
            for k, slab in enumerate(pack(transforms_group(items, gram, ys, zs))):
                t[k] = slab
            gram_copy().wait_send()
            pl.semaphore_wait(ready, 3)
            each_side(0, start)
            each_direct(0, start)

            await_halo(0)
            gram[1] = edge[0, 1] + halo[0, 0]
            gram[0] = edge[0, 0] + halo[0, 1]
            items = [outside_item(0, 0), item(0)]
            for k, m in enumerate(transforms_group(items, gram, ys, zs)):
                t[5 + k] = m.astype(BF16)
            for back in (6, 4, 2, 1):
                late(back).start()
            each_side(7, arrived)

        @pl.when(lag == last - 1)
        def _():
            pl.semaphore_wait(barrier, 1)
            gram_copy().wait_recv()
            maps = transforms_group([item(r) for r in EVEN_REGIONS], gram, ys, zs)
            for k, slab in enumerate(pack(maps)):
                t[7 + k] = slab
            pl.semaphore_wait(ready, 3)
            each_side(7, start)
            each_direct(7, start)
            each_side(0, arrived)

        @pl.when(lag < last - 1)
        def _():
            pl.semaphore_wait(barrier, 2 + (lag >= 4).astype(jnp.int32))
            pl.semaphore_signal(
                ready, inc=1, device_id={"lag": last - 1 + odd}, device_id_type=MESH)
            for parity, own, other in ((1, 0, 7), (0, 7, 0)):
                @pl.when(odd == parity)
                def _(parity=parity, own=own, other=other):
                    for k in range(len(PIECES)):
                        direct(k, own, 2).wait_recv()

                        @pl.when(lag >= 4)
                        def _(k=k):
                            direct(k, own, 2).start()

                        side(k, own).start()
                    each_side(other, arrived)

        for regions, first in ((ODD_REGIONS, 0), (EVEN_REGIONS, 7)):
            for r, m in zip(regions, unpack([t[first + k].astype(F32) for k in range(5)])):
                tf[r + 1] = m

        @pl.loop(1, COLS // 16)
        def _(group):
            for i in range(16):
                analyse(group * 16 + i, here * REG - 1, near, weight, tf, sc, sc)

        @pl.when(is_last)
        def _():
            each_direct(0, sent)
            each_side(0, sent)
            for back in (6, 4, 2, 1):
                late(back).wait_send()

        @pl.when(lag == last - 1)
        def _():
            late(1).wait_recv()
            each_direct(7, sent)
            each_side(7, sent)

        @pl.when(lag < last - 1)
        def _():
            for parity, own in ((1, 0), (0, 7)):
                @pl.when(odd == parity)
                def _(parity=parity, own=own):
                    late(1).wait_recv()
                    if parity == 1:
                        late(1).start()
                    each_side(own, sent)

                    @pl.when(lag >= 4)
                    def _():
                        for k in range(len(PIECES)):
                            direct(k, own, 2).wait_send()

                    if parity == 1:
                        late(1).wait_send()

        t_out[0] = t[5].astype(F32)
        t_out[1] = t[6].astype(F32)
        t_out[2] = tf[2]
        t_out[3] = tf[3]

    return kernel


def transforms_call(lags, spaces, *operands):
    vmem = pl.BlockSpec(memory_space=pltpu.VMEM)
    hbm = pl.BlockSpec(memory_space=pltpu.HBM)
    dma = pltpu.SemaphoreType.DMA
    return pl.pallas_call(
        make_transform_kernel(lags, spaces),
        out_shape=(
            jax.ShapeDtypeStruct((4, M, 128), F32),
            jax.ShapeDtypeStruct((COLS, 128, 128), BF16),
        ),
        in_specs=[hbm] * 8,
        out_specs=(vmem, vmem),
        scratch_shapes=[
            pltpu.VMEM((LEV, M, COLS), BF16),
            pltpu.VMEM((NOBS, LEV), BF16),
            pltpu.VMEM((NOBS, COLS), F32),
            pltpu.VMEM((NOBS, COLS), F32),
            pltpu.VMEM((REG, M), jnp.int32),
            pltpu.SMEM((REG,), F32),
            pltpu.SMEM((COLS,), jnp.int32),
            pltpu.SMEM((COLS,), F32),
            pltpu.VMEM((REG + 2, M, 128), F32),
            pltpu.VMEM((WIDTH * 128, KB), BF16),
            pltpu.VMEM((REG, KB), F32),
            pltpu.VMEM((REG, KB), F32),
            pltpu.VMEM((2, 2, MX, 128), F32),
            pltpu.VMEM((2, 2, MX, 128), F32),
            pltpu.VMEM((REG + 2, MX, 128), F32),
            pltpu.VMEM((SLABS, M, 128), BF16),
            pltpu.VMEM((8, M, 256), BF16),
            pltpu.VMEM((8, M, 256), BF16),
            dma((7,)), dma((4,)), dma((2,)), dma((2,)), dma, dma,
            dma((2, 3)), dma((2,)), dma((2,)), dma((2,)), dma((4,)), dma,
            pltpu.SemaphoreType.REGULAR,
        ],
        compiler_params=pltpu.CompilerParams(
            collective_id=0, has_side_effects=True, vmem_limit_bytes=24 * 2**20),
    )(*(pltpu.with_memory_space_constraint(x, pltpu.HBM) for x in operands))


def analysis_kernel(s, t, near, weight, out, o, ov, o_sem):
    base = lax.axis_index("space") * REG - 1
    for c in range(2 * WIDTH):
        analyse(c, base, near, weight, t, s, o)

    def store(k):
        first = k * 16
        count = min(16, LEV - first)
        return pltpu.make_async_copy(
            ov.at[pl.ds(first, count)], out.at[pl.ds(first, count)], o_sem.at[k])

    for k in range(8):
        first, stop = k * 16, min(k * 16 + 16, LEV)
        part = [ref[:, first : first + 16, :M] for ref in (o, s.at[pl.ds(16, COLS - 16)])]
        turned = jnp.transpose(jnp.concatenate(part, axis=0), (1, 2, 0))
        ov[first:stop] = turned[: stop - first]
        store(k).start()
    for k in range(8):
        store(k).wait()


def analysis_call(s, t, near, weight):
    vmem = pl.BlockSpec(memory_space=pltpu.VMEM)
    hbm = pl.BlockSpec(memory_space=pltpu.HBM)
    smem = pl.BlockSpec(memory_space=pltpu.SMEM)
    return pl.pallas_call(
        analysis_kernel,
        out_shape=jax.ShapeDtypeStruct((LEV, M, COLS), BF16),
        in_specs=[vmem, vmem, smem, smem],
        out_specs=hbm,
        scratch_shapes=[
            pltpu.VMEM((2 * WIDTH, 128, 128), BF16),
            pltpu.VMEM((LEV, M, COLS), BF16),
            pltpu.SemaphoreType.DMA((8,)),
        ],
        compiler_params=pltpu.CompilerParams(vmem_limit_bytes=24 * 2**20),
    )(s, t, near, weight)


def per_device(
    states, obs_weights, observations, obs_precision, resample_index, blend_weight,
    stencil_region, stencil_weight,
):
    st = jnp.transpose(states[0], (1, 0, 2))
    t, s = transforms_call(
        lax.axis_size("lag"), lax.axis_size("space"),
        st, obs_weights, observations, obs_precision, resample_index, blend_weight,
        stencil_region, stencil_weight)
    out = analysis_call(s, t, stencil_region, stencil_weight)
    return jnp.transpose(out, (1, 0, 2))[None]


def solution(mesh):
    in_specs = (
        P("lag", None, None, "space"), P(), P(None, "space"), P(None, "space"),
        P("space", None), P("space"), P("space"), P("space"),
    )
    return jax.shard_map(
        per_device, mesh=mesh, in_specs=in_specs, out_specs=P("lag", None, None, "space"),
        check_vma=False)
```

```python
import math

import jax
import jax.numpy as jnp
from jax import lax
from jax.experimental import pallas as pl
from jax.experimental.pallas import tpu as pltpu
from jax.sharding import PartitionSpec as P

M = 80
LEV = 127
NOBS = 24
COLS = 128
WIDTH = 8
REG = 16
NS_ITERS = 8
KB = 256
MX = 96
F32 = jnp.float32
BF16 = jnp.bfloat16
MESH = pl.DeviceIdType.MESH

TAPER = [
    [math.exp(-0.5 * ((q * WIDTH + k - (3 * WIDTH - 1) / 2.0) / WIDTH) ** 2) for k in range(WIDTH)]
    for q in range(3)
]


def split(x):
    high = x.astype(BF16)
    return high, (x - high.astype(F32)).astype(BF16)


def halves(x):
    high, low = split(x)
    return jnp.concatenate([high, low], axis=1)


def product(a, b):
    gap = jnp.zeros((128 - M, 256), BF16)
    out = jnp.dot(a, jnp.concatenate([b, gap, b, gap], axis=0), preferred_element_type=F32)
    return out[:, :128] + out[:, 128:]


def pair_rows(value, spread, chosen):
    first = value.astype(BF16)
    rest = value - first.astype(F32)
    second = rest.astype(BF16)
    third = (rest - second.astype(F32)).astype(BF16)
    dims = (((0,), (0,)), ((), ()))
    total = lax.dot_general(first, spread, dims, preferred_element_type=F32)
    total += lax.dot_general(second, spread, dims, preferred_element_type=F32)
    total += lax.dot_general(third, spread, dims, preferred_element_type=F32)
    return jnp.sum(jnp.where(chosen, total, 0.0).reshape(REG, WIDTH, KB), axis=1)


def prepare(w, y, pr, wb, yrow, rrow):
    row = lax.broadcasted_iota(jnp.int32, (NOBS, KB), 0)
    lane = lax.broadcasted_iota(jnp.int32, (NOBS, KB), 1)
    spread = jnp.where((lane % NOBS == row) & (lane < WIDTH * NOBS), 1.0, 0.0).astype(BF16)
    row = lax.broadcasted_iota(jnp.int32, (COLS, KB), 0)
    lane = lax.broadcasted_iota(jnp.int32, (COLS, KB), 1)
    chosen = lane // NOBS == row % WIDTH
    yrow[...] = pair_rows(y[...], spread, chosen)
    rrow[...] = pair_rows(jnp.sqrt(pr[...]), spread, chosen)
    wide = lax.dot_general(w[...], spread, (((0,), (0,)), ((), ())), preferred_element_type=F32)
    wide = jnp.concatenate([wide, jnp.zeros((1, KB), F32)], axis=0)
    for k in range(WIDTH):
        wb[k * 128 : (k + 1) * 128] = jnp.where(lane // NOBS == k, wide, 0.0).astype(BF16)


def scaled_blocks(regions, sc, wb, yrow, rrow):
    rows = []
    for r in regions:
        turned = jnp.transpose(sc[pl.ds(r * WIDTH, WIDTH)], (0, 2, 1))[:, :M]
        rows.append(jnp.concatenate([turned[k] for k in range(WIDTH)], axis=1))
    out = jnp.dot(jnp.concatenate(rows, axis=0), wb[...], preferred_element_type=F32)
    top = lax.broadcasted_iota(jnp.int32, (MX - M, KB), 0) == 0
    blocks = []
    for k, r in enumerate(regions):
        obs = out[k * M : (k + 1) * M]
        mean = jnp.sum(obs, axis=0, keepdims=True) * (1.0 / M)
        innovation = jnp.where(top, yrow[pl.ds(r, 1), :] - mean, 0.0)
        blocks.append(
            jnp.concatenate([obs - mean, innovation], axis=0) * rrow[pl.ds(r, 1), :]
        )
    return blocks


def block_terms(x, parts):
    left = split(x)
    across = jnp.concatenate([x, jnp.zeros((128 - MX, KB), F32)], axis=0).T
    gap = jnp.zeros((KB - WIDTH * NOBS, 128), F32)
    terms = {}
    for q in parts:
        tapered = [across[k * NOBS : (k + 1) * NOBS] * TAPER[q][k] for k in range(WIDTH)]
        terms[q] = (*left, halves(jnp.concatenate(tapered + [gap], axis=0)))
    return terms


def gram_of(terms):
    high, low, right = zip(*terms)
    right = jnp.concatenate(right, axis=0)
    out = jnp.dot(jnp.concatenate(high, axis=1), right, preferred_element_type=F32)
    out2 = jnp.dot(jnp.concatenate(low, axis=1), right[:, :128], preferred_element_type=F32)
    return out[:, :128] + out[:, 128:] + out2


def region_gram(r, blocks):
    return gram_of([blocks[r - 1 + q][q] for q in range(3)])


def transforms_group(items, gram, ys, zs):
    row = lax.broadcasted_iota(jnp.int32, (M, 128), 0)
    col = lax.broadcasted_iota(jnp.int32, (M, 128), 1)
    eye = (row == col).astype(F32)
    count = len(items)
    norms = []
    for k, (slot, _, _) in enumerate(items):
        cross = jnp.where(col < M, gram[slot, :M, :], 0.0)
        square = jnp.sum(cross * cross, axis=0, keepdims=True)
        norm = 1.0 + jnp.sqrt(jnp.sum(square, axis=1, keepdims=True)) * (1.0 / (M - 1))
        norms.append(norm)
        y = (eye + cross * (1.0 / (M - 1))) / norm
        e = halves(1.5 * eye - 0.5 * y)
        ys[k] = halves(product(halves(y), e))
        zs[k] = e

    @pl.loop(0, NS_ITERS - 2)
    def _(sweep):
        factors = [halves(1.5 * eye - 0.5 * product(zs[k], ys[k])) for k in range(count)]
        for k in range(count):
            both = product(jnp.concatenate([ys[k], zs[k]], axis=0), factors[k])
            ys[k] = halves(both[:M])
            zs[k] = halves(both[M:])

    result = []
    for k, (slot, drawn_row, share) in enumerate(items):
        e = halves(1.5 * eye - 0.5 * product(zs[k], ys[k]))
        root = product(zs[k], e) / jnp.sqrt(norms[k])
        drive = gram[slot, :M, M : M + 1]
        half = jnp.sum(root * drive, axis=0, keepdims=True)
        mean_weight = jnp.sum(root * half, axis=1, keepdims=True) * (1.0 / (M - 1))
        weights = mean_weight + root
        etkf = 1.0 / M + weights - jnp.sum(weights, axis=0, keepdims=True) * (1.0 / M)
        drawn = (drawn_row == row).astype(F32)
        result.append((1.0 - share) * etkf + share * drawn)
    return result


def pack(maps):
    lane = lax.broadcasted_iota(jnp.int32, (M, 128), 1)
    a, b, c, d, e, f, g, h = maps

    def tail(first, second=None, cut=128):
        return first if second is None else jnp.where(lane < cut, first, second)

    spare = (
        pltpu.roll(f, 80, 1),
        tail(pltpu.roll(f, 32, 1), pltpu.roll(g, 112, 1), 112),
        pltpu.roll(g, 64, 1),
        tail(pltpu.roll(g, 16, 1), pltpu.roll(h, 96, 1), 96),
        pltpu.roll(h, 48, 1),
    )
    return [
        jnp.where(lane < M, kept, extra).astype(BF16)
        for kept, extra in zip((a, b, c, d, e), spare)
    ]


def unpack(slabs):
    lane = lax.broadcasted_iota(jnp.int32, (M, 128), 1)
    a, b, c, d, e = slabs
    f = jnp.where(lane < 48, pltpu.roll(a, 48, 1), pltpu.roll(b, 96, 1))
    g = jnp.where(
        lane < 16, pltpu.roll(b, 16, 1),
        jnp.where(lane < 64, pltpu.roll(c, 64, 1), pltpu.roll(d, 112, 1)))
    h = jnp.where(lane < 32, pltpu.roll(d, 32, 1), pltpu.roll(e, 80, 1))
    return [a, b, c, d, e, f, g, h]


ODD_REGIONS = (12, 13, 14, 15, 16, 1, 2, 3)
LATE_REGIONS = (-1, 0)
EVEN_REGIONS = (4, 5, 6, 7, 8, 9, 10, 11)
SLABS = 12
PIECES = ((0, 3), (3, 2))
LEVEL_CHUNKS = ((0, 32), (32, 32), (64, 32), (96, 31))


def make_transform_kernel(lags, spaces):
    last = lags - 1

    def kernel(
        st_hbm, w_hbm, y_hbm, pr_hbm, resample_hbm, blend_hbm, t_out, sc,
        st, w, y, pr, resample, blend,
        wb, yrow, rrow, edge, halo, gram, t, ys, zs,
        in_sem, st_sem, x_send, x_recv, g_send, g_recv,
        p_next, p_side, own_recv, other_recv, f_send, f_recv, ready,
    ):
        lag = lax.axis_index("lag")
        here = lax.axis_index("space")
        odd = lax.rem(lag, 2)
        sibling = lag + 1 - 2 * odd
        has_left, has_right = here > 0, here < spaces - 1
        left, right = here - 1, here + 1
        barrier = pltpu.get_barrier_semaphore()
        is_last = lag == last

        def greet(where):
            pl.semaphore_signal(barrier, inc=1, device_id=where, device_id_type=MESH)

        greet({"lag": sibling})

        @pl.when(lag >= last - 1)
        def _():
            for back in (6, 4, 2):
                greet({"lag": lag - back})

        @pl.when(is_last)
        def _():
            @pl.when(has_left)
            def _():
                greet({"space": left})

            @pl.when(has_right)
            def _():
                greet({"space": right})

        def level_copy(k):
            first, count = LEVEL_CHUNKS[k]
            return pltpu.make_async_copy(
                st_hbm.at[pl.ds(first, count)], st.at[pl.ds(first, count)], st_sem.at[k])

        small = [
            pltpu.make_async_copy(src, dst, in_sem.at[k])
            for k, (src, dst) in enumerate(
                ((w_hbm, w), (y_hbm, y), (pr_hbm, pr), (resample_hbm, resample), (blend_hbm, blend)))
        ]
        for copy in small:
            copy.start()
        for k in range(len(LEVEL_CHUNKS)):
            level_copy(k).start()
        for copy in small:
            copy.wait()

        def columns_first():
            gap = jnp.zeros((1, M, COLS), BF16)
            for k, (first, count) in enumerate(LEVEL_CHUNKS):
                level_copy(k).wait()
                for j in range(first, first + count, 16):
                    part = st[j : min(j + 16, LEV)]
                    if j + 16 > LEV:
                        part = jnp.concatenate([part, gap], axis=0)
                    sc[:, j : j + 16, :M] = jnp.transpose(part, (2, 0, 1))

        def side(k, first):
            ref = t.at[pl.ds(first + PIECES[k][0], PIECES[k][1])]
            return pltpu.make_async_remote_copy(
                src_ref=ref, dst_ref=ref, send_sem=p_side.at[k], recv_sem=other_recv.at[k],
                device_id={"lag": sibling}, device_id_type=MESH)

        def direct(k, first, back):
            ref = t.at[pl.ds(first + PIECES[k][0], PIECES[k][1])]
            return pltpu.make_async_remote_copy(
                src_ref=ref, dst_ref=ref, send_sem=p_next.at[k, back // 2 - 1],
                recv_sem=own_recv.at[k], device_id={"lag": lag - back}, device_id_type=MESH)

        def late(back):
            ref = t.at[pl.ds(5, 2)]
            return pltpu.make_async_remote_copy(
                src_ref=ref, dst_ref=ref, send_sem=f_send.at[back // 2], recv_sem=f_recv,
                device_id={"lag": lag - back}, device_id_type=MESH)

        def each_direct(first, act):
            for back in (6, 4, 2):
                for k in range(len(PIECES)):
                    act(direct(k, first, back))

        def each_side(first, act):
            for k in range(len(PIECES)):
                act(side(k, first))

        def start(copy):
            copy.start()

        def sent(copy):
            copy.wait_send()

        def arrived(copy):
            copy.wait_recv()

        def block_copy(k, where):
            return pltpu.make_async_remote_copy(
                src_ref=edge.at[k], dst_ref=halo.at[1 - k], send_sem=x_send.at[k],
                recv_sem=x_recv.at[1 - k], device_id={"space": where}, device_id_type=MESH)

        def gram_copy():
            ref = gram.at[pl.ds(5, 8)]
            return pltpu.make_async_remote_copy(
                src_ref=ref, dst_ref=ref, send_sem=g_send, recv_sem=g_recv,
                device_id={"lag": sibling}, device_id_type=MESH)

        def drawn_row(r):
            return resample[r : r + 1, :]

        def wide_row(r):
            return jnp.concatenate([drawn_row(r), jnp.full((1, 48), -1, jnp.int32)], axis=1)

        def item(r):
            return (r + 1, wide_row(r), blend[r])

        def with_extras(partial, r):
            values = jnp.concatenate(
                [drawn_row(r).astype(F32), jnp.zeros((1, 128 - M), F32)], axis=1)
            which = lax.broadcasted_iota(jnp.int32, (MX, 128), 0)
            return jnp.where(
                which == M + 1, values, jnp.where(which == M + 2, blend[r], partial))

        def await_halo(k):
            there, where = ((has_left, left), (has_right, right))[k]

            @pl.when(there)
            def _():
                block_copy(1 - k, where).wait_recv()
                block_copy(k, where).wait_send()

            @pl.when(jnp.logical_not(there))
            def _():
                halo[k] = jnp.zeros((2, MX, 128), F32)

        def outside_item(k, slot):
            drawn = halo[k, 1, M + 1 : M + 2, :].astype(jnp.int32)
            return (slot, drawn, halo[k, 1, M + 2 : M + 3, :])

        sides = ((0, has_left, left), (1, has_right, right))

        @pl.when(is_last)
        def _():
            prepare(w, y, pr, wb, yrow, rrow)

        columns_first()

        @pl.when(is_last)
        def _():

            ends = scaled_blocks((0, 1, REG - 1, REG - 2), sc, wb, yrow, rrow)
            blocks = {}
            for r, x in zip((0, 1, 15, 14), ends):
                blocks[r] = block_terms(x, (0, 1, 2))
            edge[0, 0] = gram_of([blocks[0][2]])
            edge[0, 1] = with_extras(gram_of([blocks[0][1], blocks[1][2]]), 0)
            edge[1, 0] = gram_of([blocks[15][0]])
            edge[1, 1] = with_extras(gram_of([blocks[14][0], blocks[15][1]]), REG - 1)
            pl.semaphore_wait(
                barrier, 1 + has_left.astype(jnp.int32) + has_right.astype(jnp.int32))
            for k, there, where in sides:
                @pl.when(there)
                def _(k=k, where=where):
                    block_copy(k, where).start()

            inner = tuple(range(3, 13))
            for r, x in zip(inner, scaled_blocks(inner, sc, wb, yrow, rrow)):
                blocks[r] = block_terms(x, (0, 1, 2))
            for r in EVEN_REGIONS:
                gram[r + 1] = region_gram(r, blocks)
            gram_copy().start()
            for r, x in zip((2, 13), scaled_blocks((2, 13), sc, wb, yrow, rrow)):
                blocks[r] = block_terms(x, (0, 1, 2))
            for r in (1, 2, 3, 12, 13, 14):
                gram[r + 1] = region_gram(r, blocks)

            await_halo(1)
            gram[REG] = edge[1, 1] + halo[1, 0]
            gram[REG + 1] = edge[1, 0] + halo[1, 1]

            items = [outside_item(1, 17) if r == 16 else item(r) for r in ODD_REGIONS]
            for k, slab in enumerate(pack(transforms_group(items, gram, ys, zs))):
                t[k] = slab
            gram_copy().wait_send()
            pl.semaphore_wait(ready, 3)
            each_side(0, start)
            each_direct(0, start)

            await_halo(0)
            gram[1] = edge[0, 1] + halo[0, 0]
            gram[0] = edge[0, 0] + halo[0, 1]
            items = [outside_item(0, 0), item(0)]
            for k, m in enumerate(transforms_group(items, gram, ys, zs)):
                t[5 + k] = m.astype(BF16)
            for back in (6, 4, 2, 1):
                late(back).start()
            each_side(7, arrived)
            each_direct(0, sent)
            each_side(0, sent)
            for back in (6, 4, 2, 1):
                late(back).wait_send()

        @pl.when(lag == last - 1)
        def _():
            pl.semaphore_wait(barrier, 1)
            gram_copy().wait_recv()
            maps = transforms_group([item(r) for r in EVEN_REGIONS], gram, ys, zs)
            for k, slab in enumerate(pack(maps)):
                t[7 + k] = slab
            pl.semaphore_wait(ready, 3)
            each_side(7, start)
            each_direct(7, start)
            each_side(0, arrived)
            late(1).wait_recv()
            each_direct(7, sent)
            each_side(7, sent)

        @pl.when(lag < last - 1)
        def _():
            pl.semaphore_wait(barrier, 2)
            pl.semaphore_signal(
                ready, inc=1, device_id={"lag": last - 1 + odd}, device_id_type=MESH)
            for parity, own, other in ((1, 0, 7), (0, 7, 0)):
                @pl.when(odd == parity)
                def _(parity=parity, own=own, other=other):
                    for k in range(len(PIECES)):
                        direct(k, own, 2).wait_recv()
                        side(k, own).start()
                    each_side(other, arrived)
                    late(1).wait_recv()
                    if parity == 1:
                        late(1).start()
                    each_side(own, sent)
                    if parity == 1:
                        late(1).wait_send()

        t_out[...] = t[...]

    return kernel


def transforms_call(lags, spaces, st, w, y, pr, resample, blend):
    vmem = pl.BlockSpec(memory_space=pltpu.VMEM)
    hbm = pl.BlockSpec(memory_space=pltpu.HBM)
    dma = pltpu.SemaphoreType.DMA
    return pl.pallas_call(
        make_transform_kernel(lags, spaces),
        out_shape=(
            jax.ShapeDtypeStruct((SLABS, M, 128), BF16),
            jax.ShapeDtypeStruct((COLS, 128, 128), BF16),
        ),
        in_specs=[hbm] * 6,
        out_specs=(vmem, vmem),
        scratch_shapes=[
            pltpu.VMEM((LEV, M, COLS), BF16),
            pltpu.VMEM((NOBS, LEV), BF16),
            pltpu.VMEM((NOBS, COLS), F32),
            pltpu.VMEM((NOBS, COLS), F32),
            pltpu.VMEM((REG, M), jnp.int32),
            pltpu.SMEM((REG,), F32),
            pltpu.VMEM((WIDTH * 128, KB), BF16),
            pltpu.VMEM((REG, KB), F32),
            pltpu.VMEM((REG, KB), F32),
            pltpu.VMEM((2, 2, MX, 128), F32),
            pltpu.VMEM((2, 2, MX, 128), F32),
            pltpu.VMEM((REG + 2, MX, 128), F32),
            pltpu.VMEM((SLABS, M, 128), BF16),
            pltpu.VMEM((8, M, 256), BF16),
            pltpu.VMEM((8, M, 256), BF16),
            dma((5,)), dma((4,)), dma((2,)), dma((2,)), dma, dma,
            dma((2, 3)), dma((2,)), dma((2,)), dma((2,)), dma((4,)), dma,
            pltpu.SemaphoreType.REGULAR,
        ],
        compiler_params=pltpu.CompilerParams(
            collective_id=0, has_side_effects=True, vmem_limit_bytes=24 * 2**20),
    )(*(pltpu.with_memory_space_constraint(x, pltpu.HBM) for x in (st, w, y, pr, resample, blend)))


def analysis_kernel(s, t, near, weight, out, tf, o, ov, o_sem):
    base = lax.axis_index("space") * REG - 1
    slabs = [t[k].astype(F32) for k in range(SLABS)]
    maps = unpack(slabs[:5]) + slabs[5:7] + unpack(slabs[7:])
    for r, m in zip(ODD_REGIONS + LATE_REGIONS + EVEN_REGIONS, maps):
        tf[r + 1] = m

    def column(c):
        share = weight[c]
        maps = (share * tf[c // WIDTH + 1] + (1.0 - share) * tf[near[c] - base]).astype(BF16)
        o[c] = jnp.dot(s[c, :, :M], maps, preferred_element_type=F32).astype(BF16)

    for c in range(COLS):
        column(c)

    def store(k):
        first = k * 16
        count = min(16, LEV - first)
        return pltpu.make_async_copy(
            ov.at[pl.ds(first, count)], out.at[pl.ds(first, count)], o_sem.at[k])

    for k in range(8):
        first, stop = k * 16, min(k * 16 + 16, LEV)
        turned = jnp.transpose(o[:, first : first + 16, :M], (1, 2, 0))
        ov[first:stop] = turned[: stop - first]
        store(k).start()
    for k in range(8):
        store(k).wait()


def analysis_call(s, t, near, weight):
    vmem = pl.BlockSpec(memory_space=pltpu.VMEM)
    hbm = pl.BlockSpec(memory_space=pltpu.HBM)
    smem = pl.BlockSpec(memory_space=pltpu.SMEM)
    return pl.pallas_call(
        analysis_kernel,
        out_shape=jax.ShapeDtypeStruct((LEV, M, COLS), BF16),
        in_specs=[vmem, vmem, smem, smem],
        out_specs=hbm,
        scratch_shapes=[
            pltpu.VMEM((REG + 2, M, 128), F32),
            pltpu.VMEM((COLS, 128, 128), BF16),
            pltpu.VMEM((LEV, M, COLS), BF16),
            pltpu.SemaphoreType.DMA((8,)),
        ],
        compiler_params=pltpu.CompilerParams(vmem_limit_bytes=24 * 2**20),
    )(s, t, near, weight)


def per_device(
    states, obs_weights, observations, obs_precision, resample_index, blend_weight,
    stencil_region, stencil_weight,
):
    st = jnp.transpose(states[0], (1, 0, 2))
    t, s = transforms_call(
        lax.axis_size("lag"), lax.axis_size("space"),
        st, obs_weights, observations, obs_precision, resample_index, blend_weight)
    out = analysis_call(s, t, stencil_region, stencil_weight)
    return jnp.transpose(out, (1, 0, 2))[None]


def solution(mesh):
    in_specs = (
        P("lag", None, None, "space"), P(), P(None, "space"), P(None, "space"),
        P("space", None), P("space"), P("space"), P("space"),
    )
    return jax.shard_map(
        per_device, mesh=mesh, in_specs=in_specs, out_specs=P("lag", None, None, "space"),
        check_vma=False)
```

```python
import math

import jax
import jax.numpy as jnp
from jax import lax
from jax.experimental import pallas as pl
from jax.experimental.pallas import tpu as pltpu
from jax.sharding import PartitionSpec as P

M = 80
LEV = 127
NOBS = 24
COLS = 128
WIDTH = 8
REG = 16
NS_ITERS = 8
KB = 256
MX = 96
F32 = jnp.float32
BF16 = jnp.bfloat16
MESH = pl.DeviceIdType.MESH

TAPER = [
    [math.exp(-0.5 * ((q * WIDTH + k - (3 * WIDTH - 1) / 2.0) / WIDTH) ** 2) for k in range(WIDTH)]
    for q in range(3)
]


def split(x):
    high = x.astype(BF16)
    return high, (x - high.astype(F32)).astype(BF16)


def halves(x):
    high, low = split(x)
    return jnp.concatenate([high, low], axis=1)


def product(a, b):
    gap = jnp.zeros((128 - M, 256), BF16)
    out = jnp.dot(a, jnp.concatenate([b, gap, b, gap], axis=0), preferred_element_type=F32)
    return out[:, :128] + out[:, 128:]


def pair_rows(value, spread, chosen):
    first = value.astype(BF16)
    rest = value - first.astype(F32)
    second = rest.astype(BF16)
    third = (rest - second.astype(F32)).astype(BF16)
    dims = (((0,), (0,)), ((), ()))
    total = lax.dot_general(first, spread, dims, preferred_element_type=F32)
    total += lax.dot_general(second, spread, dims, preferred_element_type=F32)
    total += lax.dot_general(third, spread, dims, preferred_element_type=F32)
    return jnp.sum(jnp.where(chosen, total, 0.0).reshape(REG, WIDTH, KB), axis=1)


def prepare(w, y, pr, wb, yrow, rrow):
    row = lax.broadcasted_iota(jnp.int32, (NOBS, KB), 0)
    lane = lax.broadcasted_iota(jnp.int32, (NOBS, KB), 1)
    spread = jnp.where((lane % NOBS == row) & (lane < WIDTH * NOBS), 1.0, 0.0).astype(BF16)
    row = lax.broadcasted_iota(jnp.int32, (COLS, KB), 0)
    lane = lax.broadcasted_iota(jnp.int32, (COLS, KB), 1)
    chosen = lane // NOBS == row % WIDTH
    yrow[...] = pair_rows(y[...], spread, chosen)
    rrow[...] = pair_rows(jnp.sqrt(pr[...]), spread, chosen)
    wide = lax.dot_general(w[...], spread, (((0,), (0,)), ((), ())), preferred_element_type=F32)
    wide = jnp.concatenate([wide, jnp.zeros((1, KB), F32)], axis=0)
    for k in range(WIDTH):
        wb[k * 128 : (k + 1) * 128] = jnp.where(lane // NOBS == k, wide, 0.0).astype(BF16)


def scaled_blocks(regions, sc, wb, yrow, rrow):
    rows = []
    for r in regions:
        turned = jnp.transpose(sc[pl.ds(r * WIDTH, WIDTH)], (0, 2, 1))[:, :M]
        rows.append(jnp.concatenate([turned[k] for k in range(WIDTH)], axis=1))
    out = jnp.dot(jnp.concatenate(rows, axis=0), wb[...], preferred_element_type=F32)
    top = lax.broadcasted_iota(jnp.int32, (MX - M, KB), 0) == 0
    blocks = []
    for k, r in enumerate(regions):
        obs = out[k * M : (k + 1) * M]
        mean = jnp.sum(obs, axis=0, keepdims=True) * (1.0 / M)
        innovation = jnp.where(top, yrow[pl.ds(r, 1), :] - mean, 0.0)
        blocks.append(
            jnp.concatenate([obs - mean, innovation], axis=0) * rrow[pl.ds(r, 1), :]
        )
    return blocks


def block_terms(x, parts):
    left = split(x)
    across = jnp.concatenate([x, jnp.zeros((128 - MX, KB), F32)], axis=0).T
    gap = jnp.zeros((KB - WIDTH * NOBS, 128), F32)
    terms = {}
    for q in parts:
        tapered = [across[k * NOBS : (k + 1) * NOBS] * TAPER[q][k] for k in range(WIDTH)]
        terms[q] = (*left, halves(jnp.concatenate(tapered + [gap], axis=0)))
    return terms


def gram_of(terms):
    high, low, right = zip(*terms)
    right = jnp.concatenate(right, axis=0)
    out = jnp.dot(jnp.concatenate(high, axis=1), right, preferred_element_type=F32)
    out2 = jnp.dot(jnp.concatenate(low, axis=1), right[:, :128], preferred_element_type=F32)
    return out[:, :128] + out[:, 128:] + out2


def region_gram(r, blocks):
    return gram_of([blocks[r - 1 + q][q] for q in range(3)])


def transforms_group(items, gram, ys, zs):
    row = lax.broadcasted_iota(jnp.int32, (M, 128), 0)
    col = lax.broadcasted_iota(jnp.int32, (M, 128), 1)
    eye = (row == col).astype(F32)
    count = len(items)
    norms = []
    for k, (slot, _, _) in enumerate(items):
        cross = jnp.where(col < M, gram[slot, :M, :], 0.0)
        square = jnp.sum(cross * cross, axis=0, keepdims=True)
        norm = 1.0 + jnp.sqrt(jnp.sum(square, axis=1, keepdims=True)) * (1.0 / (M - 1))
        norms.append(norm)
        y = (eye + cross * (1.0 / (M - 1))) / norm
        e = halves(1.5 * eye - 0.5 * y)
        ys[k] = halves(product(halves(y), e))
        zs[k] = e

    @pl.loop(0, NS_ITERS - 2)
    def _(sweep):
        factors = [halves(1.5 * eye - 0.5 * product(zs[k], ys[k])) for k in range(count)]
        for k in range(count):
            both = product(jnp.concatenate([ys[k], zs[k]], axis=0), factors[k])
            ys[k] = halves(both[:M])
            zs[k] = halves(both[M:])

    result = []
    for k, (slot, drawn_row, share) in enumerate(items):
        e = halves(1.5 * eye - 0.5 * product(zs[k], ys[k]))
        root = product(zs[k], e) / jnp.sqrt(norms[k])
        drive = gram[slot, :M, M : M + 1]
        half = jnp.sum(root * drive, axis=0, keepdims=True)
        mean_weight = jnp.sum(root * half, axis=1, keepdims=True) * (1.0 / (M - 1))
        weights = mean_weight + root
        etkf = 1.0 / M + weights - jnp.sum(weights, axis=0, keepdims=True) * (1.0 / M)
        drawn = (drawn_row == row).astype(F32)
        result.append((1.0 - share) * etkf + share * drawn)
    return result


def pack(maps):
    lane = lax.broadcasted_iota(jnp.int32, (M, 128), 1)
    a, b, c, d, e, f, g, h = maps

    def tail(first, second=None, cut=128):
        return first if second is None else jnp.where(lane < cut, first, second)

    spare = (
        pltpu.roll(f, 80, 1),
        tail(pltpu.roll(f, 32, 1), pltpu.roll(g, 112, 1), 112),
        pltpu.roll(g, 64, 1),
        tail(pltpu.roll(g, 16, 1), pltpu.roll(h, 96, 1), 96),
        pltpu.roll(h, 48, 1),
    )
    return [
        jnp.where(lane < M, kept, extra).astype(BF16)
        for kept, extra in zip((a, b, c, d, e), spare)
    ]


def unpack(slabs):
    lane = lax.broadcasted_iota(jnp.int32, (M, 128), 1)
    a, b, c, d, e = slabs
    f = jnp.where(lane < 48, pltpu.roll(a, 48, 1), pltpu.roll(b, 96, 1))
    g = jnp.where(
        lane < 16, pltpu.roll(b, 16, 1),
        jnp.where(lane < 64, pltpu.roll(c, 64, 1), pltpu.roll(d, 112, 1)))
    h = jnp.where(lane < 32, pltpu.roll(d, 32, 1), pltpu.roll(e, 80, 1))
    return [a, b, c, d, e, f, g, h]


ODD_REGIONS = (12, 13, 14, 15, 16, 1, 2, 3)
LATE_REGIONS = (-1, 0)
EVEN_REGIONS = (4, 5, 6, 7, 8, 9, 10, 11)
SLABS = 12
PIECES = ((0, 3), (3, 2))
LEVEL_CHUNKS = ((0, 32), (32, 32), (64, 32), (96, 31))


def make_transform_kernel(lags, spaces):
    last = lags - 1

    def kernel(
        st_hbm, w_hbm, y_hbm, pr_hbm, resample_hbm, blend_hbm, t_out, sc,
        st, w, y, pr, resample, blend,
        wb, yrow, rrow, edge, halo, gram, t, ys, zs,
        in_sem, st_sem, x_send, x_recv, g_send, g_recv,
        p_next, p_side, own_recv, other_recv, f_send, f_recv, ready,
    ):
        lag = lax.axis_index("lag")
        here = lax.axis_index("space")
        odd = lax.rem(lag, 2)
        sibling = lag + 1 - 2 * odd
        has_left, has_right = here > 0, here < spaces - 1
        left, right = here - 1, here + 1
        barrier = pltpu.get_barrier_semaphore()
        is_last = lag == last

        def greet(where):
            pl.semaphore_signal(barrier, inc=1, device_id=where, device_id_type=MESH)

        greet({"lag": sibling})

        @pl.when(lag >= last - 1)
        def _():
            for back in (6, 4, 2):
                greet({"lag": lag - back})

        @pl.when(is_last)
        def _():
            @pl.when(has_left)
            def _():
                greet({"space": left})

            @pl.when(has_right)
            def _():
                greet({"space": right})

        def level_copy(k):
            first, count = LEVEL_CHUNKS[k]
            return pltpu.make_async_copy(
                st_hbm.at[pl.ds(first, count)], st.at[pl.ds(first, count)], st_sem.at[k])

        small = [
            pltpu.make_async_copy(src, dst, in_sem.at[k])
            for k, (src, dst) in enumerate(
                ((w_hbm, w), (y_hbm, y), (pr_hbm, pr), (resample_hbm, resample), (blend_hbm, blend)))
        ]
        for copy in small:
            copy.start()
        for k in range(len(LEVEL_CHUNKS)):
            level_copy(k).start()
        for copy in small:
            copy.wait()

        def columns_first():
            gap = jnp.zeros((1, M, COLS), BF16)
            for k, (first, count) in enumerate(LEVEL_CHUNKS):
                level_copy(k).wait()
                for j in range(first, first + count, 16):
                    part = st[j : min(j + 16, LEV)]
                    if j + 16 > LEV:
                        part = jnp.concatenate([part, gap], axis=0)
                    sc[:, j : j + 16, :M] = jnp.transpose(part, (2, 0, 1))

        def side(k, first):
            ref = t.at[pl.ds(first + PIECES[k][0], PIECES[k][1])]
            return pltpu.make_async_remote_copy(
                src_ref=ref, dst_ref=ref, send_sem=p_side.at[k], recv_sem=other_recv.at[k],
                device_id={"lag": sibling}, device_id_type=MESH)

        def direct(k, first, back):
            ref = t.at[pl.ds(first + PIECES[k][0], PIECES[k][1])]
            return pltpu.make_async_remote_copy(
                src_ref=ref, dst_ref=ref, send_sem=p_next.at[k, back // 2 - 1],
                recv_sem=own_recv.at[k], device_id={"lag": lag - back}, device_id_type=MESH)

        def late(back):
            ref = t.at[pl.ds(5, 2)]
            return pltpu.make_async_remote_copy(
                src_ref=ref, dst_ref=ref, send_sem=f_send.at[back // 2], recv_sem=f_recv,
                device_id={"lag": lag - back}, device_id_type=MESH)

        def each_direct(first, act):
            for back in (6, 4, 2):
                for k in range(len(PIECES)):
                    act(direct(k, first, back))

        def each_side(first, act):
            for k in range(len(PIECES)):
                act(side(k, first))

        def start(copy):
            copy.start()

        def sent(copy):
            copy.wait_send()

        def arrived(copy):
            copy.wait_recv()

        def block_copy(k, where):
            return pltpu.make_async_remote_copy(
                src_ref=edge.at[k], dst_ref=halo.at[1 - k], send_sem=x_send.at[k],
                recv_sem=x_recv.at[1 - k], device_id={"space": where}, device_id_type=MESH)

        def gram_copy():
            ref = gram.at[pl.ds(5, 8)]
            return pltpu.make_async_remote_copy(
                src_ref=ref, dst_ref=ref, send_sem=g_send, recv_sem=g_recv,
                device_id={"lag": sibling}, device_id_type=MESH)

        def drawn_row(r):
            return resample[r : r + 1, :]

        def wide_row(r):
            return jnp.concatenate([drawn_row(r), jnp.full((1, 48), -1, jnp.int32)], axis=1)

        def item(r):
            return (r + 1, wide_row(r), blend[r])

        def with_extras(partial, r):
            values = jnp.concatenate(
                [drawn_row(r).astype(F32), jnp.zeros((1, 128 - M), F32)], axis=1)
            which = lax.broadcasted_iota(jnp.int32, (MX, 128), 0)
            return jnp.where(
                which == M + 1, values, jnp.where(which == M + 2, blend[r], partial))

        def await_halo(k):
            there, where = ((has_left, left), (has_right, right))[k]

            @pl.when(there)
            def _():
                block_copy(1 - k, where).wait_recv()
                block_copy(k, where).wait_send()

            @pl.when(jnp.logical_not(there))
            def _():
                halo[k] = jnp.zeros((2, MX, 128), F32)

        def outside_item(k, slot):
            drawn = halo[k, 1, M + 1 : M + 2, :].astype(jnp.int32)
            return (slot, drawn, halo[k, 1, M + 2 : M + 3, :])

        sides = ((0, has_left, left), (1, has_right, right))

        @pl.when(is_last)
        def _():
            prepare(w, y, pr, wb, yrow, rrow)

        columns_first()

        @pl.when(is_last)
        def _():

            ends = scaled_blocks((0, 1, REG - 1, REG - 2), sc, wb, yrow, rrow)
            blocks = {}
            for r, x in zip((0, 1, 15, 14), ends):
                blocks[r] = block_terms(x, (0, 1, 2))
            edge[0, 0] = gram_of([blocks[0][2]])
            edge[0, 1] = with_extras(gram_of([blocks[0][1], blocks[1][2]]), 0)
            edge[1, 0] = gram_of([blocks[15][0]])
            edge[1, 1] = with_extras(gram_of([blocks[14][0], blocks[15][1]]), REG - 1)
            pl.semaphore_wait(
                barrier, 1 + has_left.astype(jnp.int32) + has_right.astype(jnp.int32))
            for k, there, where in sides[::-1]:
                @pl.when(there)
                def _(k=k, where=where):
                    block_copy(k, where).start()

            inner = tuple(range(3, 13))
            for r, x in zip(inner, scaled_blocks(inner, sc, wb, yrow, rrow)):
                blocks[r] = block_terms(x, (0, 1, 2))
            for r in EVEN_REGIONS:
                gram[r + 1] = region_gram(r, blocks)
            gram_copy().start()
            for r, x in zip((2, 13), scaled_blocks((2, 13), sc, wb, yrow, rrow)):
                blocks[r] = block_terms(x, (0, 1, 2))
            for r in (1, 2, 3, 12, 13, 14):
                gram[r + 1] = region_gram(r, blocks)

            await_halo(1)
            gram[REG] = edge[1, 1] + halo[1, 0]
            gram[REG + 1] = edge[1, 0] + halo[1, 1]

            items = [outside_item(1, 17) if r == 16 else item(r) for r in ODD_REGIONS]
            for k, slab in enumerate(pack(transforms_group(items, gram, ys, zs))):
                t[k] = slab
            gram_copy().wait_send()
            pl.semaphore_wait(ready, 3)
            each_side(0, start)
            each_direct(0, start)

            await_halo(0)
            gram[1] = edge[0, 1] + halo[0, 0]
            gram[0] = edge[0, 0] + halo[0, 1]
            items = [outside_item(0, 0), item(0)]
            for k, m in enumerate(transforms_group(items, gram, ys, zs)):
                t[5 + k] = m.astype(BF16)
            for back in (6, 4, 2, 1):
                late(back).start()
            each_side(7, arrived)
            each_direct(0, sent)
            each_side(0, sent)
            for back in (6, 4, 2, 1):
                late(back).wait_send()

        @pl.when(lag == last - 1)
        def _():
            pl.semaphore_wait(barrier, 1)
            gram_copy().wait_recv()
            maps = transforms_group([item(r) for r in EVEN_REGIONS], gram, ys, zs)
            for k, slab in enumerate(pack(maps)):
                t[7 + k] = slab
            pl.semaphore_wait(ready, 3)
            each_side(7, start)
            each_direct(7, start)
            each_side(0, arrived)
            late(1).wait_recv()
            each_direct(7, sent)
            each_side(7, sent)

        @pl.when(lag < last - 1)
        def _():
            pl.semaphore_wait(barrier, 2)
            pl.semaphore_signal(
                ready, inc=1, device_id={"lag": last - 1 + odd}, device_id_type=MESH)
            for parity, own, other in ((1, 0, 7), (0, 7, 0)):
                @pl.when(odd == parity)
                def _(parity=parity, own=own, other=other):
                    for k in range(len(PIECES)):
                        direct(k, own, 2).wait_recv()
                        side(k, own).start()
                    each_side(other, arrived)
                    late(1).wait_recv()
                    if parity == 1:
                        late(1).start()
                    each_side(own, sent)
                    if parity == 1:
                        late(1).wait_send()

        t_out[...] = t[...]

    return kernel


def transforms_call(lags, spaces, st, w, y, pr, resample, blend):
    vmem = pl.BlockSpec(memory_space=pltpu.VMEM)
    hbm = pl.BlockSpec(memory_space=pltpu.HBM)
    dma = pltpu.SemaphoreType.DMA
    return pl.pallas_call(
        make_transform_kernel(lags, spaces),
        out_shape=(
            jax.ShapeDtypeStruct((SLABS, M, 128), BF16),
            jax.ShapeDtypeStruct((COLS, 128, 128), BF16),
        ),
        in_specs=[hbm] * 6,
        out_specs=(vmem, vmem),
        scratch_shapes=[
            pltpu.VMEM((LEV, M, COLS), BF16),
            pltpu.VMEM((NOBS, LEV), BF16),
            pltpu.VMEM((NOBS, COLS), F32),
            pltpu.VMEM((NOBS, COLS), F32),
            pltpu.VMEM((REG, M), jnp.int32),
            pltpu.SMEM((REG,), F32),
            pltpu.VMEM((WIDTH * 128, KB), BF16),
            pltpu.VMEM((REG, KB), F32),
            pltpu.VMEM((REG, KB), F32),
            pltpu.VMEM((2, 2, MX, 128), F32),
            pltpu.VMEM((2, 2, MX, 128), F32),
            pltpu.VMEM((REG + 2, MX, 128), F32),
            pltpu.VMEM((SLABS, M, 128), BF16),
            pltpu.VMEM((8, M, 256), BF16),
            pltpu.VMEM((8, M, 256), BF16),
            dma((5,)), dma((4,)), dma((2,)), dma((2,)), dma, dma,
            dma((2, 3)), dma((2,)), dma((2,)), dma((2,)), dma((4,)), dma,
            pltpu.SemaphoreType.REGULAR,
        ],
        compiler_params=pltpu.CompilerParams(
            collective_id=0, has_side_effects=True, vmem_limit_bytes=24 * 2**20),
    )(*(pltpu.with_memory_space_constraint(x, pltpu.HBM) for x in (st, w, y, pr, resample, blend)))


def analysis_kernel(s, t, near, weight, out, tf, o, ov, o_sem):
    base = lax.axis_index("space") * REG - 1
    slabs = [t[k].astype(F32) for k in range(SLABS)]
    maps = unpack(slabs[:5]) + slabs[5:7] + unpack(slabs[7:])
    for r, m in zip(ODD_REGIONS + LATE_REGIONS + EVEN_REGIONS, maps):
        tf[r + 1] = m

    def column(c):
        share = weight[c]
        maps = (share * tf[c // WIDTH + 1] + (1.0 - share) * tf[near[c] - base]).astype(BF16)
        o[c] = jnp.dot(s[c, :, :M], maps, preferred_element_type=F32).astype(BF16)

    for c in range(COLS):
        column(c)

    def store(k):
        first = k * 16
        count = min(16, LEV - first)
        return pltpu.make_async_copy(
            ov.at[pl.ds(first, count)], out.at[pl.ds(first, count)], o_sem.at[k])

    for k in range(8):
        first, stop = k * 16, min(k * 16 + 16, LEV)
        turned = jnp.transpose(o[:, first : first + 16, :M], (1, 2, 0))
        ov[first:stop] = turned[: stop - first]
        store(k).start()
    for k in range(8):
        store(k).wait()


def analysis_call(s, t, near, weight):
    vmem = pl.BlockSpec(memory_space=pltpu.VMEM)
    hbm = pl.BlockSpec(memory_space=pltpu.HBM)
    smem = pl.BlockSpec(memory_space=pltpu.SMEM)
    return pl.pallas_call(
        analysis_kernel,
        out_shape=jax.ShapeDtypeStruct((LEV, M, COLS), BF16),
        in_specs=[vmem, vmem, smem, smem],
        out_specs=hbm,
        scratch_shapes=[
            pltpu.VMEM((REG + 2, M, 128), F32),
            pltpu.VMEM((COLS, 128, 128), BF16),
            pltpu.VMEM((LEV, M, COLS), BF16),
            pltpu.SemaphoreType.DMA((8,)),
        ],
        compiler_params=pltpu.CompilerParams(vmem_limit_bytes=24 * 2**20),
    )(s, t, near, weight)


def per_device(
    states, obs_weights, observations, obs_precision, resample_index, blend_weight,
    stencil_region, stencil_weight,
):
    st = jnp.transpose(states[0], (1, 0, 2))
    t, s = transforms_call(
        lax.axis_size("lag"), lax.axis_size("space"),
        st, obs_weights, observations, obs_precision, resample_index, blend_weight)
    out = analysis_call(s, t, stencil_region, stencil_weight)
    return jnp.transpose(out, (1, 0, 2))[None]


def solution(mesh):
    in_specs = (
        P("lag", None, None, "space"), P(), P(None, "space"), P(None, "space"),
        P("space", None), P("space"), P("space"), P("space"),
    )
    return jax.shard_map(
        per_device, mesh=mesh, in_specs=in_specs, out_specs=P("lag", None, None, "space"),
        check_vma=False)
```
